32 devices in a mesh: groups: 2 (over y), tok: 4 (over z), ffn: 2 (over x), rep: 2 (over core).
Axes of the slice: x: 2, y: 2, z: 4, core: 2. Of those that a mesh axis runs over, the one named last changes fastest.
Arguments:
- queries: bfloat16 [64, 4096], P(('groups', 'tok', 'ffn'), 'rep'), parts along dimension 0, may hold values from -100 to 100
- new_key: bfloat16 [64, 512], P(('groups', 'tok', 'ffn'), 'rep'), parts along dimension 0, may hold values from -100 to 100
- new_value: bfloat16 [64, 512], P(('groups', 'tok', 'ffn'), 'rep'), parts along dimension 0, may hold values from -6 to 6
- key_cache: bfloat16 [64, 512, 512], P(('groups', 'tok', 'ffn'), None, 'rep'), parts along dimension 0, may hold values from -4 to 4
- value_cache: bfloat16 [64, 512, 512], P(('groups', 'tok', 'ffn'), None, 'rep'), parts along dimension 0, may hold values from -6 to 6
- lengths: int32 [64], P(('groups', 'tok', 'ffn')), parts along dimension 0, may hold values from 1 to 512
- slot_of: int32 [64], P('groups'), parts along dimension 0, may hold values from 0 to 31, each once
- residual_in: bfloat16 [64, 8192], P('groups', 'tok'), parts along dimension 0, may hold values from -100 to 100
- out_weight: bfloat16 [4, 1024, 8192], P('rep', 'ffn', 'tok'), may hold values from -0.5 to 0.5
- norm_gain: float32 [8192], P('tok'), may hold values from 0.5 to 1.5
- gate_weight: bfloat16 [8192, 14336], P('tok', ('ffn', 'rep')), may hold values from -0.0625 to 0.0625
- up_weight: bfloat16 [8192, 14336], P('tok', ('ffn', 'rep')), may hold values from -0.0625 to 0.0625
- down_weight: bfloat16 [14336, 8192], P(('ffn', 'rep'), 'tok'), may hold values from -0.046875 to 0.046875
Outputs:
- layer_out: bfloat16 [64, 8192], P(('groups', 'ffn', 'rep'), 'tok'), parts along dimension 0
The draws below stay inside these ranges and needn't reach their ends.
There are 2 independent parts, one for each index of `groups`. The reference program is written for one: setup_inputs(seed, part) draws one part's arguments, and reference() takes and returns one part's arrays. A program takes and returns all parts, laid end to end along the dimension named above; an argument that names none is the same for every part. Nothing has to cross between parts.
Inputs may be any that keep to these rules, and one draw needn't show every extreme that they name: Each of 0 to 31 once; request i's queries, keys, values and length sit in row slot_of[i].
All inputs are finite; a program needn't handle non-finite values.
Results may differ from the reference program's by a relative error of at most 0.01.
Values may be sent and summed in bfloat16 or wider, within the bound.
No kernel may reach another device: no remote copies, remote signals or barrier semaphores. Data moves between devices by JAX's collectives and lax.ppermute only.
A program may use at most 128 MiB of HBM per device.

```python
import jax
import jax.numpy as jnp
from jax import lax

D = 8192
FF = 14336
HEADS = 32
KV_HEADS = 4
HEAD_DIM = 128
CTX = 512
GROUP = 8
REQS = 32


def shared_keys(key):
    cache_keys = jnp.clip(jax.random.normal(jax.random.fold_in(key, 11), (REQS, CTX, KV_HEADS * HEAD_DIM), jnp.float32), -4.0, 4.0)
    return cache_keys


def draw_key_cache(key, part):
    cache_keys = shared_keys(key)
    return cache_keys.astype(jnp.bfloat16)


def draw_queries(key, part):
    key = jax.random.fold_in(key, 21)
    result = jnp.clip(jax.random.normal(key, (REQS, HEADS * HEAD_DIM), jnp.float32), -5.0, 5.0)
    return result.astype(jnp.bfloat16)


def draw_new_key(key, part):
    key = jax.random.fold_in(key, 31)
    result = jnp.clip(jax.random.normal(key, (REQS, KV_HEADS * HEAD_DIM), jnp.float32), -5.0, 5.0)
    return result.astype(jnp.bfloat16)


def draw_lengths(key, part):
    key = jax.random.fold_in(key, 51)
    first_key, second_key = jax.random.split(key)
    drawn = jax.random.randint(first_key, (REQS,), 1, CTX + 1)
    longest = jax.random.randint(second_key, (), 0, REQS)
    return jnp.where(jnp.arange(REQS) == longest, CTX, drawn).astype(jnp.int32)


def draw_residual_in(key, part):
    key = jax.random.fold_in(key, 41)
    row_key, col_key, noise_key = jax.random.split(key, 3)
    columns = 0.5 * 3.0 ** (jnp.arange(D, dtype=jnp.float32) / D)
    columns = columns[None, :] * 10.0 ** jax.random.uniform(col_key, (1, D), jnp.float32, -0.5, 0.5)
    row_scale = 10.0 ** jax.random.uniform(row_key, (REQS, 1), jnp.float32, -0.5, 0.5)
    noise = jnp.clip(jax.random.normal(noise_key, (REQS, D), jnp.float32), -5.0, 5.0)
    return (noise * row_scale * columns).astype(jnp.bfloat16)


def block_scale(key, extent, shards, smallest, top_value):
    factor_of = 1.0
    for dim, parts in shards:
        draws = jax.random.uniform(jax.random.fold_in(jax.random.fold_in(key, 6), dim), (parts,), jnp.float32, smallest / len(shards), top_value / len(shards))
        factor_of = factor_of * jnp.repeat(jnp.exp(draws), extent[dim] // parts).reshape((-1,) + (1,) * (len(extent) - 1 - dim))
    return factor_of


def scatter_about(rng, extent, scale, bound, shards=(), kind=jnp.bfloat16):
    values = jax.random.normal(rng, extent, jnp.float32) * scale
    if len(shards) > 0:
        values = block_scale(rng, extent, shards, -0.22, 0.18) * values
    return jnp.clip(values, min=-bound, max=bound).astype(kind)


def setup_inputs(seed: int = 0, part: int = 0) -> dict:
    key_list = jax.random.split(jax.random.key(seed), 14)
    part_splits = jax.random.split(jax.random.fold_in(key_list[13], part), 14)
    return {
        "queries": draw_queries(jax.random.fold_in(jax.random.fold_in(key_list[13], part), 71), part),
        "new_key": draw_new_key(jax.random.fold_in(jax.random.fold_in(key_list[13], part), 71), part),
        "new_value": scatter_about(part_splits[2], (REQS, KV_HEADS * HEAD_DIM), 1.0, 6.0, ((0, 8), (1, 2))),
        "key_cache": draw_key_cache(jax.random.fold_in(jax.random.fold_in(key_list[13], part), 71), part),
        "value_cache": scatter_about(part_splits[4], (REQS, CTX, KV_HEADS * HEAD_DIM), 1.0, 6.0, ((0, 8), (2, 2))),
        "lengths": draw_lengths(jax.random.fold_in(jax.random.fold_in(key_list[13], part), 71), part),
        "slot_of": jax.random.permutation(part_splits[6], REQS).astype(jnp.int32),
        "residual_in": draw_residual_in(jax.random.fold_in(jax.random.fold_in(key_list[13], part), 71), part),
        "out_weight": scatter_about(key_list[8], (KV_HEADS, GROUP * HEAD_DIM, D), (HEADS * HEAD_DIM // 32) ** -0.5, 0.5, ((0, 2), (1, 2), (2, 4))),
        "norm_gain": jnp.clip(1.0 + 0.1 * jax.random.normal(key_list[9], (D,), jnp.float32), 0.5, 1.5),
        "gate_weight": scatter_about(key_list[10], (D, FF), D ** -0.5, 0.0625, ((0, 4), (1, 4))),
        "up_weight": scatter_about(key_list[11], (D, FF), D ** -0.5, 0.0625, ((0, 4), (1, 4))),
        "down_weight": scatter_about(key_list[12], (FF, D), FF ** -0.5, 0.046875, ((0, 4), (1, 4))),
    }


def reference(queries, new_key, new_value, key_cache, value_cache, lengths, slot_of, residual_in, out_weight, norm_gain, gate_weight, up_weight, down_weight):
    slots = queries.shape[0]
    group_size = HEADS // KV_HEADS
    score_scale = HEAD_DIM ** (-0.5)
    heads_q = queries.astype(jnp.float32).reshape(slots, KV_HEADS, group_size, HEAD_DIM)
    keys_all = key_cache.astype(jnp.float32).reshape(slots, CTX, KV_HEADS, HEAD_DIM)
    values_all = value_cache.astype(jnp.float32).reshape(slots, CTX, KV_HEADS, HEAD_DIM)
    own_key = new_key.astype(jnp.float32).reshape(slots, KV_HEADS, HEAD_DIM)
    own_value = new_value.astype(jnp.float32).reshape(slots, KV_HEADS, HEAD_DIM)
    scores = jnp.einsum('rgqd,rpgd->rgqp', heads_q, keys_all) * score_scale
    own_score = jnp.einsum('rgqd,rgd->rgq', heads_q, own_key) * score_scale
    positions = jnp.arange(CTX, dtype=jnp.int32)
    live_mask = positions[None, :] < lengths[:, None]
    masked = jnp.where(live_mask[:, None, None, :], scores, -jnp.inf)
    row_top = jnp.maximum(lax.optimization_barrier(jnp.max(masked, axis=-1)), own_score)
    exp_cache = jnp.exp(masked - row_top[..., None])
    exp_own = jnp.exp(own_score - row_top)
    weight_sum = lax.optimization_barrier(jnp.sum(exp_cache, axis=-1)) + exp_own
    prob_cache = (exp_cache / weight_sum[..., None]).astype(jnp.bfloat16)
    prob_own = (exp_own / weight_sum).astype(jnp.bfloat16)
    attended = jnp.einsum('rgqp,rpgd->rgqd', prob_cache.astype(jnp.float32), values_all)
    attended = attended + prob_own.astype(jnp.float32)[..., None] * own_value[:, :, None, :]
    attended = attended.astype(jnp.bfloat16).reshape(slots, HEADS * HEAD_DIM)
    ordered = attended[slot_of]
    projected = jnp.dot(ordered, out_weight.reshape(HEADS * HEAD_DIM, D), preferred_element_type=jnp.float32)
    mid_state = (residual_in.astype(jnp.float32) + projected).astype(jnp.bfloat16)
    mid_float = mid_state.astype(jnp.float32)
    inv_rms = lax.rsqrt(lax.optimization_barrier(jnp.mean(mid_float * mid_float, axis=1)) + 1e-05)
    normed = (mid_float * inv_rms[:, None] * norm_gain[None, :]).astype(jnp.bfloat16)
    gate = jnp.dot(normed, gate_weight, preferred_element_type=jnp.float32)
    up_sum = jnp.dot(normed, up_weight, preferred_element_type=jnp.float32)
    hidden = (jax.nn.silu(gate) * up_sum).astype(jnp.bfloat16)
    down_sum = jnp.dot(hidden, down_weight, preferred_element_type=jnp.float32)
    return (mid_float + down_sum).astype(jnp.bfloat16)
```

```python
import functools

import jax
import jax.numpy as jnp
from jax import lax
from jax.experimental import pallas as pl
from jax.experimental.pallas import tpu as pltpu
from jax.sharding import PartitionSpec as P

HEAD_DIM = 128
F32 = jnp.float32
BF16 = jnp.bfloat16
MIB = 2**20
VMEM = pl.BlockSpec(memory_space=pltpu.VMEM)
SMEM = pl.BlockSpec(memory_space=pltpu.SMEM)
HBM = pl.BlockSpec(memory_space=pl.ANY)


def swap(extent, step):
    return [(a, a ^ step) for a in range(extent)]


def column_step(width):
    for step in (896, 512, 256, 128):
        if width % step == 0:
            return step
    return width


def attend(
    copies, lens, queries, new_key, new_value, keys, values, out, key_buf, value_buf, sems
):
    slots, span, width = key_buf.shape
    kv_here = width // HEAD_DIM
    group = queries.shape[1] // width
    rows = group * slots
    loads = []
    for s in range(slots):
        loads.append(pltpu.make_async_copy(keys.at[s], key_buf.at[s], sems.at[0, s]))
    for s in range(slots):
        loads.append(pltpu.make_async_copy(values.at[s], value_buf.at[s], sems.at[1, s]))
    for load in loads:
        load.start()
    scale = HEAD_DIM ** (-0.5)
    slot_id = lax.rem(lax.broadcasted_iota(jnp.int32, (rows, 1), 0), slots)
    live_len = jnp.zeros((rows, 1), jnp.int32)
    for s in range(slots):
        live_len = jnp.where(slot_id == s, lens[s], live_len)
    live = lax.broadcasted_iota(jnp.int32, (rows, span), 1) < live_len
    q_all = queries[...].astype(F32)
    own_k = new_key[...].astype(F32)
    own_v = new_value[...].astype(F32)
    heads_q, own_score = [], []
    for g in range(kv_here):
        cols = slice(g * HEAD_DIM, (g + 1) * HEAD_DIM)
        first = g * group
        q = jnp.concatenate(
            [
                q_all[:, (first + h) * HEAD_DIM : (first + h + 1) * HEAD_DIM]
                for h in range(group)
            ],
            axis=0,
        )
        k = jnp.concatenate([own_k[:, cols]] * group, axis=0)
        own_score.append(jnp.sum(q * k, axis=1, keepdims=True) * scale)
        heads_q.append(q.astype(BF16))
    scores = [jnp.zeros((rows, span), F32) for _ in range(kv_here)]
    for s in range(slots):
        loads[s].wait()
        for g in range(kv_here):
            here = lax.dot_general(
                heads_q[g],
                key_buf[s, :, g * HEAD_DIM : (g + 1) * HEAD_DIM],
                (((1,), (1,)), ((), ())),
                preferred_element_type=F32,
            )
            scores[g] = jnp.where(slot_id == s, here, scores[g])
    probs, totals = [], []
    for g in range(kv_here):
        masked = jnp.where(live, scores[g] * scale, -jnp.inf)
        top = jnp.maximum(jnp.max(masked, axis=1, keepdims=True), own_score[g])
        exp_cache = jnp.exp(masked - top)
        exp_own = jnp.exp(own_score[g] - top)
        total = jnp.sum(exp_cache, axis=1, keepdims=True) + exp_own
        probs.append((exp_cache / total).astype(BF16))
        own = jnp.concatenate(
            [own_v[:, g * HEAD_DIM : (g + 1) * HEAD_DIM]] * group, axis=0
        )
        totals.append((exp_own / total).astype(BF16).astype(F32) * own)
    for s in range(slots):
        loads[slots + s].wait()
        for g in range(kv_here):
            here = jnp.where(slot_id == s, probs[g], jnp.zeros_like(probs[g]))
            totals[g] += jnp.dot(
                here,
                value_buf[s, :, g * HEAD_DIM : (g + 1) * HEAD_DIM],
                preferred_element_type=F32,
            )
    width_out = out.shape[2]
    heads_out = width_out // HEAD_DIM
    parts = group // heads_out
    for f in range(parts):
        block = jnp.concatenate(
            [
                jnp.concatenate(
                    [totals[g][h * slots : (h + 1) * slots] for g in range(kv_here)], axis=0
                )
                for h in range(f * heads_out, (f + 1) * heads_out)
            ],
            axis=1,
        ).astype(BF16)
        for t in range(copies):
            out[t * parts + f] = block


def project(slots, slot_of, heads, weight, out):
    requests = slot_of.shape[1]
    blocks, rows, width = heads.shape
    kv_here = weight.shape[0]
    table = heads[...].astype(F32).reshape(blocks * rows, width).astype(BF16)
    slot = slot_of[...]
    where_from = (slot // slots) * rows + lax.rem(slot, slots)
    row = lax.broadcasted_iota(jnp.int32, (blocks * rows, requests), 0)
    ordered = []
    for g in range(kv_here):
        pick = (row == where_from + g * slots).astype(F32).astype(BF16)
        ordered.append(
            lax.dot_general(
                pick, table, (((0,), (0,)), ((), ())), preferred_element_type=F32
            ).astype(BF16)
        )
    step = column_step(out.shape[1])
    for c in range(0, out.shape[1], step):
        total = jnp.zeros((requests, step), F32)
        for g in range(kv_here):
            total += jnp.dot(
                ordered[g], weight[g, :, c : c + step], preferred_element_type=F32
            )
        out[:, c : c + step] = total.astype(BF16)


def gate_and_up(others, *refs):
    place, residual, gain, here = refs[:4]
    arrived = refs[4 : 4 + others]
    gate_weight, up_weight, mid_out = refs[4 + others : 7 + others]
    parts = refs[7 + others : -2]
    ordered, squares = refs[-2:]
    blocks, rows, _ = ordered.shape
    width = gate_weight.shape[1]
    mid = residual[...].astype(F32) + here[...].astype(F32)
    for other in arrived:
        mid += other[...].astype(F32)
    mid = mid.astype(BF16).astype(F32)
    share = mid_out.shape[1]
    for j in range(mid_out.shape[0]):
        mid_out[j] = mid[j * share : (j + 1) * share].astype(BF16)
    square = jnp.broadcast_to(jnp.sum(mid * mid, axis=1, keepdims=True), (mid.shape[0], 128))
    scaled = mid * gain[...]
    for k in range(blocks):
        ordered[k] = scaled[k * rows : (k + 1) * rows]
        squares[k] = square[k * rows : (k + 1) * rows]
    mine = place[0]
    left = jnp.concatenate([ordered[mine ^ k] for k in range(blocks)], axis=0).astype(BF16)
    lane = lax.broadcasted_iota(jnp.int32, (rows, 128), 1)
    for k in range(blocks):
        value = squares[mine ^ k]
        high = value.astype(BF16).astype(F32)
        middle = (value - high).astype(BF16).astype(F32)
        low = value - high - middle
        stat = jnp.where(lane == 0, high, jnp.where(lane == 1, middle, low))
        parts[k][:, 2 * width :] = jnp.where(lane < 3, stat, 0.0).astype(BF16)
    step = column_step(width)
    for base, weight in ((0, gate_weight), (width, up_weight)):
        for c in range(0, width, step):
            total = jnp.dot(left, weight[:, c : c + step], preferred_element_type=F32)
            for k in range(blocks):
                parts[k][:, base + c : base + c + step] = total[
                    k * rows : (k + 1) * rows
                ].astype(BF16)


def activate(features, *refs):
    out = refs[-1]
    width = out.shape[1]
    total = refs[0][...].astype(F32)
    for part in refs[1:-1]:
        total += part[...].astype(F32)
    square = jnp.sum(total[:, 2 * width :], axis=1, keepdims=True)
    inv_rms = lax.rsqrt(square / features + 1e-05)
    gate = total[:, :width] * inv_rms
    up = total[:, width : 2 * width] * inv_rms
    out[...] = (gate / (1.0 + jnp.exp(-gate)) * up).astype(BF16)


def down(blocks, *refs):
    place = refs[0]
    parts = refs[1 : 1 + blocks]
    weight = refs[1 + blocks]
    outs = refs[2 + blocks : -1]
    ordered = refs[-1]
    rows = parts[0].shape[0]
    share = outs[0].shape[0]
    for k in range(blocks):
        at = pl.multiple_of((place[0] ^ k) * rows, 8)
        ordered[pl.ds(at, rows)] = parts[k][...].astype(F32)
    left = jnp.concatenate(
        [
            ordered[pl.ds(pl.multiple_of((place[1] ^ j) * share, 8), share)]
            for j in range(len(outs))
        ],
        axis=0,
    ).astype(BF16)
    width = weight.shape[1]
    step = column_step(width)
    for c in range(0, width, step):
        total = jnp.dot(left, weight[:, c : c + step], preferred_element_type=F32)
        for j, out in enumerate(outs):
            out[:, c : c + step] = total[j * share : (j + 1) * share].astype(BF16)


def finish(place, mid, *refs):
    out = refs[-1]
    total = mid[place[1]].astype(F32)
    for part in refs[:-1]:
        total += part[...].astype(F32)
    out[...] = total.astype(BF16)


def like(*shape):
    return jax.ShapeDtypeStruct(shape, BF16)


def limit(mib):
    return pltpu.CompilerParams(vmem_limit_bytes=mib * MIB)


def shards(
    queries,
    new_key,
    new_value,
    key_cache,
    value_cache,
    lengths,
    slot_of,
    residual_in,
    out_weight,
    norm_gain,
    gate_weight,
    up_weight,
    down_weight,
):
    tok, ffn, rep = (lax.axis_size(a) for a in ("tok", "ffn", "rep"))
    sums = ffn * rep
    slots, span, kv_width = key_cache.shape
    kv_here = kv_width // HEAD_DIM
    requests, features = residual_in.shape
    hidden_here = gate_weight.shape[1]
    feat_width = out_weight.shape[1]
    place = jnp.stack([lax.axis_index("tok"), lax.axis_index(("ffn", "rep"))]).astype(jnp.int32)
    in_vmem = functools.partial(pltpu.with_memory_space_constraint, memory_space=pltpu.VMEM)
    out_weight, gate_weight, up_weight, down_weight = (
        in_vmem(w) for w in (out_weight, gate_weight, up_weight, down_weight)
    )

    attended = pl.pallas_call(
        functools.partial(attend, tok),
        out_shape=like(tok * ffn, slots * kv_here, feat_width),
        in_specs=[SMEM, VMEM, VMEM, VMEM, HBM, HBM],
        out_specs=VMEM,
        scratch_shapes=[
            pltpu.VMEM(key_cache.shape, BF16),
            pltpu.VMEM(value_cache.shape, BF16),
            pltpu.SemaphoreType.DMA((2, slots)),
        ],
        compiler_params=limit(8),
        name="attend",
    )(lengths, queries, new_key, new_value, key_cache, value_cache)
    gathered = lax.all_to_all(attended, ("tok", "ffn"), 0, 0)

    partial = pl.pallas_call(
        functools.partial(project, slots),
        out_shape=like(requests, features),
        in_specs=[VMEM, VMEM, VMEM],
        out_specs=VMEM,
        compiler_params=limit(8),
        name="project",
    )(slot_of.reshape(1, requests), gathered, out_weight)
    here = partial
    for k in range(1, rep):
        here = here + lax.ppermute(partial, "rep", swap(rep, k))
    arrived = [lax.ppermute(here, "ffn", swap(ffn, k)) for k in range(1, ffn)]

    rows = requests // tok
    share = requests // sums
    mid, *parts = pl.pallas_call(
        functools.partial(gate_and_up, len(arrived)),
        out_shape=[like(sums, share, features)] + [like(rows, 2 * hidden_here + 128)] * tok,
        in_specs=[SMEM] + [VMEM] * (5 + len(arrived)),
        out_specs=[VMEM] * (1 + tok),
        scratch_shapes=[
            pltpu.VMEM((tok, rows, features), F32),
            pltpu.VMEM((tok, rows, 128), F32),
        ],
        compiler_params=limit(8),
        name="gate_and_up",
    )(place, residual_in, norm_gain.reshape(1, features), here, *arrived, gate_weight, up_weight)
    order = sorted(range(1, tok), reverse=True)
    got = [parts[0]] + [lax.ppermute(parts[k], "tok", swap(tok, k)) for k in order]

    hidden = pl.pallas_call(
        functools.partial(activate, features * tok),
        out_shape=like(rows, hidden_here),
        in_specs=[VMEM] * tok,
        out_specs=VMEM,
        compiler_params=limit(8),
        name="activate",
    )(*got)
    pieces = {k: lax.ppermute(hidden, "tok", swap(tok, k)) for k in order}

    downs = pl.pallas_call(
        functools.partial(down, tok),
        out_shape=[like(share, features)] * sums,
        in_specs=[SMEM] + [VMEM] * (1 + tok),
        out_specs=[VMEM] * sums,
        scratch_shapes=[pltpu.VMEM((requests, hidden_here), F32)],
        compiler_params=limit(8),
        name="down",
    )(place, hidden, *[pieces[k] for k in range(1, tok)], down_weight)
    order = sorted(range(1, sums), reverse=True)
    got = [downs[0]] + [lax.ppermute(downs[j], ("ffn", "rep"), swap(sums, j)) for j in order]

    return pl.pallas_call(
        finish,
        out_shape=like(share, features),
        in_specs=[SMEM] + [VMEM] * (1 + sums),
        out_specs=VMEM,
        compiler_params=limit(8),
        name="finish",
    )(place, mid, *got)


def solution(mesh):
    placed = (
        P(("groups", "tok", "ffn"), "rep"),
        P(("groups", "tok", "ffn"), "rep"),
        P(("groups", "tok", "ffn"), "rep"),
        P(("groups", "tok", "ffn"), None, "rep"),
        P(("groups", "tok", "ffn"), None, "rep"),
        P(("groups", "tok", "ffn")),
        P("groups"),
        P("groups", "tok"),
        P("rep", "ffn", "tok"),
        P("tok"),
        P("tok", ("ffn", "rep")),
        P("tok", ("ffn", "rep")),
        P(("ffn", "rep"), "tok"),
    )
    return jax.shard_map(
        shards,
        mesh=mesh,
        in_specs=placed,
        out_specs=P(("groups", "ffn", "rep"), "tok"),
        check_vma=False,
    )
```

```python
import functools

import jax
import jax.numpy as jnp
from jax import lax
from jax.experimental import pallas as pl
from jax.experimental.pallas import tpu as pltpu
from jax.sharding import PartitionSpec as P

HEAD_DIM = 128
F32 = jnp.float32
BF16 = jnp.bfloat16
MIB = 2**20
VMEM = pl.BlockSpec(memory_space=pltpu.VMEM)
SMEM = pl.BlockSpec(memory_space=pltpu.SMEM)
ANY = pl.BlockSpec(memory_space=pl.ANY)
HBM = ANY


def swap(extent, step):
    return [(a, a ^ step) for a in range(extent)]


def column_step(width):
    for step in (896, 512, 256, 128):
        if width % step == 0:
            return step
    return width


def attend(
    copies, lens_in, queries_in, new_key_in, new_value_in, keys, values, *refs
):
    count = (len(refs) - 8) // 2
    carried_in, out, carried_out = refs[:count], refs[count], refs[count + 1 : 2 * count + 1]
    lens, queries, new_key, new_value, key_buf, value_buf, sems = refs[2 * count + 1 :]
    slots, span, width = key_buf.shape
    kv_here = width // HEAD_DIM
    group = queries.shape[1] // width
    rows = group * slots
    small = [(lens_in, lens), (queries_in, queries), (new_key_in, new_key)]
    small.append((new_value_in, new_value))
    pairs = small + [(keys.at[s], key_buf.at[s]) for s in range(slots)]
    pairs += [(values.at[s], value_buf.at[s]) for s in range(slots)]
    pairs += list(zip(carried_in, carried_out))
    loads = [pltpu.make_async_copy(a, b, sems.at[i]) for i, (a, b) in enumerate(pairs)]
    for load in loads:
        load.start()
    for load in loads[: len(small)]:
        load.wait()
    loads = loads[len(small) :]
    scale = HEAD_DIM ** (-0.5)
    slot_id = lax.rem(lax.broadcasted_iota(jnp.int32, (rows, 1), 0), slots)
    live_len = jnp.zeros((rows, 1), jnp.int32)
    for s in range(slots):
        live_len = jnp.where(slot_id == s, lens[s], live_len)
    live = lax.broadcasted_iota(jnp.int32, (rows, span), 1) < live_len
    q_all = queries[...].astype(F32)
    own_k = new_key[...].astype(F32)
    own_v = new_value[...].astype(F32)
    heads_q, own_score = [], []
    for g in range(kv_here):
        cols = slice(g * HEAD_DIM, (g + 1) * HEAD_DIM)
        first = g * group
        q = jnp.concatenate(
            [
                q_all[:, (first + h) * HEAD_DIM : (first + h + 1) * HEAD_DIM]
                for h in range(group)
            ],
            axis=0,
        )
        k = jnp.concatenate([own_k[:, cols]] * group, axis=0)
        own_score.append(jnp.sum(q * k, axis=1, keepdims=True) * scale)
        heads_q.append(q.astype(BF16))
    scores = [jnp.zeros((rows, span), F32) for _ in range(kv_here)]
    for s in range(slots):
        loads[s].wait()
        for g in range(kv_here):
            here = lax.dot_general(
                heads_q[g],
                key_buf[s, :, g * HEAD_DIM : (g + 1) * HEAD_DIM],
                (((1,), (1,)), ((), ())),
                preferred_element_type=F32,
            )
            scores[g] = jnp.where(slot_id == s, here, scores[g])
    probs, totals = [], []
    for g in range(kv_here):
        masked = jnp.where(live, scores[g] * scale, -jnp.inf)
        top = jnp.maximum(jnp.max(masked, axis=1, keepdims=True), own_score[g])
        exp_cache = jnp.exp(masked - top)
        exp_own = jnp.exp(own_score[g] - top)
        total = jnp.sum(exp_cache, axis=1, keepdims=True) + exp_own
        probs.append((exp_cache / total).astype(BF16))
        own = jnp.concatenate(
            [own_v[:, g * HEAD_DIM : (g + 1) * HEAD_DIM]] * group, axis=0
        )
        totals.append((exp_own / total).astype(BF16).astype(F32) * own)
    for s in range(slots):
        loads[slots + s].wait()
        for g in range(kv_here):
            here = jnp.where(slot_id == s, probs[g], jnp.zeros_like(probs[g]))
            totals[g] += jnp.dot(
                here,
                value_buf[s, :, g * HEAD_DIM : (g + 1) * HEAD_DIM],
                preferred_element_type=F32,
            )
    width_out = out.shape[2]
    heads_out = width_out // HEAD_DIM
    parts = group // heads_out
    for f in range(parts):
        block = jnp.concatenate(
            [
                jnp.concatenate(
                    [totals[g][h * slots : (h + 1) * slots] for g in range(kv_here)], axis=0
                )
                for h in range(f * heads_out, (f + 1) * heads_out)
            ],
            axis=1,
        ).astype(BF16)
        for t in range(copies):
            out[t * parts + f] = block
    for load in loads[2 * slots :]:
        load.wait()


def fetch(first, source, *refs):
    out, sems = refs[-2:]
    rows = out.shape[0] // sems.shape[0]
    loads = []
    for i in range(sems.shape[0]):
        at = pl.ds(i * rows, rows)
        columns = pl.ds(first, out.shape[1])
        loads.append(pltpu.make_async_copy(source.at[at, columns], out.at[at], sems.at[i]))
    for load in loads:
        load.start()
    for load in loads:
        load.wait()


def project(slots, slot_of, heads, weight, out):
    requests = slot_of.shape[1]
    blocks, rows, width = heads.shape
    kv_here = weight.shape[0]
    table = heads[...].astype(F32).reshape(blocks * rows, width).astype(BF16)
    slot = slot_of[...]
    where_from = (slot // slots) * rows + lax.rem(slot, slots)
    row = lax.broadcasted_iota(jnp.int32, (blocks * rows, requests), 0)
    ordered = []
    for g in range(kv_here):
        pick = (row == where_from + g * slots).astype(F32).astype(BF16)
        ordered.append(
            lax.dot_general(
                pick, table, (((0,), (0,)), ((), ())), preferred_element_type=F32
            ).astype(BF16)
        )
    step = column_step(out.shape[1])
    for c in range(0, out.shape[1], step):
        total = jnp.zeros((requests, step), F32)
        for g in range(kv_here):
            total += jnp.dot(
                ordered[g], weight[g, :, c : c + step], preferred_element_type=F32
            )
        out[:, c : c + step] = total.astype(BF16)


def gate(others, *refs):
    place, residual, gain, here = refs[:4]
    arrived = refs[4 : 4 + others]
    weight, mid_out, left_out, stat_out = refs[4 + others : 8 + others]
    parts = refs[8 + others : -2]
    ordered, squares = refs[-2:]
    blocks, rows, _ = ordered.shape
    width = weight.shape[1]
    mid = residual[...].astype(F32) + here[...].astype(F32)
    for other in arrived:
        mid += other[...].astype(F32)
    mid = mid.astype(BF16).astype(F32)
    share = mid_out.shape[1]
    for j in range(mid_out.shape[0]):
        mid_out[j] = mid[j * share : (j + 1) * share].astype(BF16)
    square = jnp.broadcast_to(jnp.sum(mid * mid, axis=1, keepdims=True), (mid.shape[0], 128))
    scaled = mid * gain[...]
    for k in range(blocks):
        ordered[k] = scaled[k * rows : (k + 1) * rows]
        squares[k] = square[k * rows : (k + 1) * rows]
    mine = place[0]
    left = jnp.concatenate([ordered[mine ^ k] for k in range(blocks)], axis=0).astype(BF16)
    left_out[...] = left
    lane = lax.broadcasted_iota(jnp.int32, (rows, 128), 1)
    for k in range(blocks):
        value = squares[mine ^ k]
        high = value.astype(BF16).astype(F32)
        middle = (value - high).astype(BF16).astype(F32)
        low = value - high - middle
        stat = jnp.where(lane == 0, high, jnp.where(lane == 1, middle, low))
        stat = jnp.where(lane < 3, stat, 0.0).astype(BF16)
        if k < 2:
            stat_out[k] = stat
        else:
            parts[k][:, width:] = stat
    step = column_step(width)
    for c in range(0, width, step):
        total = jnp.dot(left, weight[:, c : c + step], preferred_element_type=F32)
        for k in range(blocks):
            parts[k][:, c : c + step] = total[k * rows : (k + 1) * rows].astype(BF16)


def up(left, weight, *refs):
    parts = refs[:-2]
    buf, sems = refs[-2:]
    rows, width = parts[0].shape
    step = column_step(width)
    loads = []
    for i, c in enumerate(range(0, width, step)):
        at = pl.ds(c, step)
        loads.append(pltpu.make_async_copy(weight.at[:, at], buf.at[:, at], sems.at[i]))
    for load in loads:
        load.start()
    rhs = left[...]
    for i, c in enumerate(range(0, width, step)):
        loads[i].wait()
        total = jnp.dot(rhs, buf[:, c : c + step], preferred_element_type=F32)
        for k, part in enumerate(parts):
            part[:, c : c + step] = total[k * rows : (k + 1) * rows].astype(BF16)


def join(up_part, gate_part, stat, *refs):
    out = refs[-1]
    width = up_part.shape[1]
    out[:, :width] = up_part[...]
    out[:, width : 2 * width] = gate_part[...]
    out[:, 2 * width :] = stat[1]


def activate(features, near, *refs):
    out = refs[-1]
    width = out.shape[1]
    own_up, own_gate, own_stat = refs[:3]
    both, refs = refs[3 : 2 + near], refs[2 + near : -1]
    far = len(refs) // 2
    ups, gates = refs[:far], refs[far : 2 * far]
    up_sum = own_up[...].astype(F32)
    gate_sum = own_gate[...].astype(F32)
    stat = own_stat[0].astype(F32)
    for part in both:
        up_sum += part[:, :width].astype(F32)
        gate_sum += part[:, width : 2 * width].astype(F32)
        stat += part[:, 2 * width :].astype(F32)
    for part in ups:
        up_sum += part[...].astype(F32)
    for part in gates:
        gate_sum += part[:, :width].astype(F32)
        stat += part[:, width:].astype(F32)
    square = jnp.sum(stat, axis=1, keepdims=True)
    inv_rms = lax.rsqrt(square / features + 1e-05)
    gated = gate_sum * inv_rms
    out[...] = (gated / (1.0 + jnp.exp(-gated)) * (up_sum * inv_rms)).astype(BF16)


def down(blocks, pieces, *refs):
    place = refs[0]
    parts = refs[1 : 1 + blocks]
    weights = refs[1 + blocks : 1 + blocks + pieces]
    outs = refs[1 + blocks + pieces : -1]
    ordered = refs[-1]
    rows = parts[0].shape[0]
    share = outs[0].shape[0]
    for k in range(blocks):
        at = pl.multiple_of((place[0] ^ k) * rows, 8)
        ordered[pl.ds(at, rows)] = parts[k][...].astype(F32)
    left = jnp.concatenate(
        [
            ordered[pl.ds(pl.multiple_of((place[1] ^ j) * share, 8), share)]
            for j in range(len(outs))
        ],
        axis=0,
    ).astype(BF16)
    base = 0
    for weight in weights:
        width = weight.shape[1]
        step = column_step(width)
        for c in range(0, width, step):
            total = jnp.dot(left, weight[:, c : c + step], preferred_element_type=F32)
            for j, out in enumerate(outs):
                at = base + c
                out[:, at : at + step] = total[j * share : (j + 1) * share].astype(BF16)
        base += width


def finish(place, mid, *refs):
    out = refs[-1]
    total = mid[place[1]].astype(F32)
    for part in refs[:-1]:
        total += part[...].astype(F32)
    out[...] = total.astype(BF16)


def like(*shape):
    return jax.ShapeDtypeStruct(shape, BF16)


def limit(mib):
    return pltpu.CompilerParams(vmem_limit_bytes=mib * MIB)


def fetched(source, after, first=0, width=None):
    width = width or source.shape[1]
    return pl.pallas_call(
        functools.partial(fetch, first),
        out_shape=pltpu.VMEM((source.shape[0], width), source.dtype),
        in_specs=[HBM, HBM],
        out_specs=VMEM,
        scratch_shapes=[pltpu.SemaphoreType.DMA((8,))],
        compiler_params=limit(1),
        cost_estimate=pl.CostEstimate(
            flops=0, transcendentals=0, bytes_accessed=0
        ),
        name="fetch",
    )(pltpu.with_memory_space_constraint(source, pltpu.HBM), after)


def shards(
    queries,
    new_key,
    new_value,
    key_cache,
    value_cache,
    lengths,
    slot_of,
    residual_in,
    out_weight,
    norm_gain,
    gate_weight,
    up_weight,
    down_weight,
):
    tok, ffn, rep = (lax.axis_size(a) for a in ("tok", "ffn", "rep"))
    sums = ffn * rep
    slots, span, kv_width = key_cache.shape
    kv_here = kv_width // HEAD_DIM
    requests, features = residual_in.shape
    hidden_here = gate_weight.shape[1]
    feat_width = out_weight.shape[1]
    place = jnp.stack([lax.axis_index("tok"), lax.axis_index(("ffn", "rep"))]).astype(jnp.int32)
    in_hbm = functools.partial(pltpu.with_memory_space_constraint, memory_space=pltpu.HBM)

    carried = [
        out_weight,
        slot_of.reshape(1, requests),
        residual_in,
        norm_gain.reshape(1, features),
    ]
    attended, out_weight, slot_of, residual_in, norm_gain = pl.pallas_call(
        functools.partial(attend, tok),
        out_shape=[like(tok * ffn, slots * kv_here, feat_width)]
        + [pltpu.VMEM(a.shape, a.dtype) for a in carried],
        in_specs=[HBM] * (6 + len(carried)),
        out_specs=[VMEM] * (1 + len(carried)),
        scratch_shapes=[
            pltpu.SMEM(lengths.shape, jnp.int32),
            pltpu.VMEM(queries.shape, BF16),
            pltpu.VMEM(new_key.shape, BF16),
            pltpu.VMEM(new_value.shape, BF16),
            pltpu.VMEM(key_cache.shape, BF16),
            pltpu.VMEM(value_cache.shape, BF16),
            pltpu.SemaphoreType.DMA((4 + 2 * slots + len(carried),)),
        ],
        compiler_params=limit(8),
        name="attend",
    )(
        *(
            in_hbm(a)
            for a in [lengths, queries, new_key, new_value, key_cache, value_cache] + carried
        )
    )
    gathered = lax.all_to_all(attended, ("tok", "ffn"), 0, 0)

    partial = pl.pallas_call(
        functools.partial(project, slots),
        out_shape=like(requests, features),
        in_specs=[VMEM, VMEM, VMEM],
        out_specs=VMEM,
        compiler_params=limit(8),
        name="project",
    )(slot_of, gathered, out_weight)
    here = partial
    for k in range(1, rep):
        here = here + lax.ppermute(partial, "rep", swap(rep, k))
    arrived = [lax.ppermute(here, "ffn", swap(ffn, k)) for k in range(1, ffn)]
    gate_weight = fetched(gate_weight, here)

    rows = requests // tok
    share = requests // sums
    near = min(2, tok)
    both_width = 2 * hidden_here + 128
    mid, left, stat, *gates = pl.pallas_call(
        functools.partial(gate, len(arrived)),
        out_shape=[like(sums, share, features), like(requests, features), like(near, rows, 128)]
        + [like(rows, hidden_here + (128 if k >= near else 0)) for k in range(tok)],
        in_specs=[SMEM] + [VMEM] * (4 + len(arrived)),
        out_specs=[VMEM] * (3 + tok),
        scratch_shapes=[
            pltpu.VMEM((tok, rows, features), F32),
            pltpu.VMEM((tok, rows, 128), F32),
        ],
        compiler_params=limit(8),
        name="gate",
    )(place, residual_in, norm_gain, here, *arrived, gate_weight)
    far = sorted(range(near, tok), reverse=True)
    got_gates = [lax.ppermute(gates[k], "tok", swap(tok, k)) for k in far]
    ups = pl.pallas_call(
        up,
        out_shape=[like(rows, hidden_here)] * tok,
        in_specs=[VMEM, HBM],
        out_specs=[VMEM] * tok,
        scratch_shapes=[
            pltpu.VMEM(up_weight.shape, BF16),
            pltpu.SemaphoreType.DMA((hidden_here // column_step(hidden_here),)),
        ],
        compiler_params=limit(20),
        cost_estimate=pl.CostEstimate(
            flops=0, transcendentals=0, bytes_accessed=4 * up_weight.size
        ),
        name="up",
    )(left, in_hbm(up_weight))
    got_ups = [lax.ppermute(ups[k], "tok", swap(tok, k)) for k in far]
    got_both = []
    if near > 1:
        both = pl.pallas_call(
            join,
            out_shape=like(rows, both_width),
            in_specs=[VMEM] * 3 + [ANY] * len(far),
            out_specs=VMEM,
            compiler_params=limit(4),
            name="join",
        )(ups[1], gates[1], stat, *got_gates)
        got_both.append(lax.ppermute(both, "tok", swap(tok, 1)))
    half = features // 2
    down_left = fetched(down_weight, ups[0], 0, half)

    hidden = pl.pallas_call(
        functools.partial(activate, features * tok, near),
        out_shape=like(rows, hidden_here),
        in_specs=[VMEM] * (2 + near + 2 * len(far)) + [ANY],
        out_specs=VMEM,
        compiler_params=limit(8),
        name="activate",
    )(ups[0], gates[0], stat, *got_both, *got_ups, *got_gates, down_left)
    pieces = {k: lax.ppermute(hidden, "tok", swap(tok, k)) for k in sorted(range(1, tok), reverse=True)}
    down_right = fetched(down_weight, hidden, half, half)

    downs = pl.pallas_call(
        functools.partial(down, tok, 2),
        out_shape=[like(share, features)] * sums,
        in_specs=[SMEM] + [VMEM] * (2 + tok),
        out_specs=[VMEM] * sums,
        scratch_shapes=[pltpu.VMEM((requests, hidden_here), F32)],
        compiler_params=limit(8),
        name="down",
    )(place, hidden, *[pieces[k] for k in range(1, tok)], down_left, down_right)
    order = sorted(range(1, sums), reverse=True)
    got = [downs[0]] + [lax.ppermute(downs[j], ("ffn", "rep"), swap(sums, j)) for j in order]

    return pl.pallas_call(
        finish,
        out_shape=like(share, features),
        in_specs=[SMEM] + [VMEM] * (1 + sums),
        out_specs=VMEM,
        compiler_params=limit(8),
        name="finish",
    )(place, mid, *got)


def solution(mesh):
    placed = (
        P(("groups", "tok", "ffn"), "rep"),
        P(("groups", "tok", "ffn"), "rep"),
        P(("groups", "tok", "ffn"), "rep"),
        P(("groups", "tok", "ffn"), None, "rep"),
        P(("groups", "tok", "ffn"), None, "rep"),
        P(("groups", "tok", "ffn")),
        P("groups"),
        P("groups", "tok"),
        P("rep", "ffn", "tok"),
        P("tok"),
        P("tok", ("ffn", "rep")),
        P("tok", ("ffn", "rep")),
        P(("ffn", "rep"), "tok"),
    )
    return jax.shard_map(
        shards,
        mesh=mesh,
        in_specs=placed,
        out_specs=P(("groups", "ffn", "rep"), "tok"),
        check_vma=False,
    )
```

```python
import functools

import jax
import jax.numpy as jnp
from jax import lax
from jax.experimental import pallas as pl
from jax.experimental.pallas import tpu as pltpu
from jax.sharding import PartitionSpec as P

HEAD_DIM = 128
F32 = jnp.float32
BF16 = jnp.bfloat16
MIB = 2**20
VMEM = pl.BlockSpec(memory_space=pltpu.VMEM)
SMEM = pl.BlockSpec(memory_space=pltpu.SMEM)
ANY = pl.BlockSpec(memory_space=pl.ANY)
HBM = ANY


def swap(extent, step):
    return [(a, a ^ step) for a in range(extent)]


def column_step(width):
    for step in (896, 512, 256, 128):
        if width % step == 0:
            return step
    return width


def attend(peers, lens_in, queries_in, new_key_in, new_value_in, keys, values, *refs):
    count = (len(refs) - 8 - peers) // 2
    carried_in, outs = refs[:count], refs[count : count + peers]
    carried_out = refs[count + peers : 2 * count + peers]
    lens, queries, new_key, new_value, key_buf, value_buf, shares, sems = refs[-8:]
    slots, span, width = key_buf.shape
    kv_here = width // HEAD_DIM
    group = queries.shape[1] // width
    rows = group * slots
    small = [(lens_in, lens), (queries_in, queries), (new_key_in, new_key)]
    small.append((new_value_in, new_value))
    pairs = small + [(keys.at[s], key_buf.at[s]) for s in range(slots)]
    pairs += [(values.at[s], value_buf.at[s]) for s in range(slots)]
    pairs += list(zip(carried_in, carried_out))
    loads = [pltpu.make_async_copy(a, b, sems.at[i]) for i, (a, b) in enumerate(pairs)]
    for load in loads:
        load.start()
    for load in loads[: len(small)]:
        load.wait()
    loads = loads[len(small) :]
    scale = HEAD_DIM ** (-0.5)
    slot_id = lax.rem(lax.broadcasted_iota(jnp.int32, (rows, 1), 0), slots)
    live_len = jnp.zeros((rows, 1), jnp.int32)
    for s in range(slots):
        live_len = jnp.where(slot_id == s, lens[s], live_len)
    live = lax.broadcasted_iota(jnp.int32, (rows, span), 1) < live_len
    q_all = queries[...].astype(F32)
    own_k = new_key[...].astype(F32)
    own_v = new_value[...].astype(F32)
    heads_q, own_score = [], []
    for g in range(kv_here):
        cols = slice(g * HEAD_DIM, (g + 1) * HEAD_DIM)
        first = g * group
        q = jnp.concatenate(
            [
                q_all[:, (first + h) * HEAD_DIM : (first + h + 1) * HEAD_DIM]
                for h in range(group)
            ],
            axis=0,
        )
        k = jnp.concatenate([own_k[:, cols]] * group, axis=0)
        own_score.append(jnp.sum(q * k, axis=1, keepdims=True) * scale)
        heads_q.append(q.astype(BF16))
    scores = [jnp.zeros((rows, span), F32) for _ in range(kv_here)]
    for s in range(slots):
        loads[s].wait()
        for g in range(kv_here):
            here = lax.dot_general(
                heads_q[g],
                key_buf[s, :, g * HEAD_DIM : (g + 1) * HEAD_DIM],
                (((1,), (1,)), ((), ())),
                preferred_element_type=F32,
            )
            scores[g] = jnp.where(slot_id == s, here, scores[g])
    probs, totals = [], []
    for g in range(kv_here):
        masked = jnp.where(live, scores[g] * scale, -jnp.inf)
        top = jnp.maximum(jnp.max(masked, axis=1, keepdims=True), own_score[g])
        exp_cache = jnp.exp(masked - top)
        exp_own = jnp.exp(own_score[g] - top)
        total = jnp.sum(exp_cache, axis=1, keepdims=True) + exp_own
        probs.append((exp_cache / total).astype(BF16))
        own = jnp.concatenate(
            [own_v[:, g * HEAD_DIM : (g + 1) * HEAD_DIM]] * group, axis=0
        )
        totals.append((exp_own / total).astype(BF16).astype(F32) * own)
    for s in range(slots):
        loads[slots + s].wait()
        for g in range(kv_here):
            here = jnp.where(slot_id == s, probs[g], jnp.zeros_like(probs[g]))
            totals[g] += jnp.dot(
                here,
                value_buf[s, :, g * HEAD_DIM : (g + 1) * HEAD_DIM],
                preferred_element_type=F32,
            )
    heads_out = group // peers
    for f in range(peers):
        shares[f] = jnp.concatenate(
            [
                jnp.concatenate(
                    [totals[g][h * slots : (h + 1) * slots] for g in range(kv_here)], axis=0
                )
                for h in range(f * heads_out, (f + 1) * heads_out)
            ],
            axis=1,
        )
    mine = lax.axis_index("ffn")
    for f in range(peers):
        outs[f][...] = shares[mine ^ f].astype(BF16)
    for load in loads[2 * slots :]:
        load.wait()


def stack(count, *refs):
    out = refs[-1]
    for i, ref in enumerate(refs[:count]):
        out[i] = ref[...]


def add(count, *refs):
    total = refs[0][...].astype(F32)
    for ref in refs[1:count]:
        total += ref[...].astype(F32)
    refs[-1][...] = total.astype(BF16)


def project(slots, slot_of, weight, *refs):
    refs, out = refs[:-1], refs[-1]
    requests = slot_of.shape[1]
    _, rows, width = refs[0].shape
    kv_here = weight.shape[0]
    table = [ref[...].astype(F32).reshape(ref.shape[0] * rows, width) for ref in refs]
    table = jnp.concatenate(table, axis=0).astype(BF16)
    slot = slot_of[...]
    mine = lax.axis_index(("tok", "ffn"))
    where_from = ((slot // slots) ^ mine) * rows + lax.rem(slot, slots)
    row = lax.broadcasted_iota(jnp.int32, (table.shape[0], requests), 0)
    ordered = []
    for g in range(kv_here):
        pick = (row == where_from + g * slots).astype(F32).astype(BF16)
        ordered.append(
            lax.dot_general(
                pick, table, (((0,), (0,)), ((), ())), preferred_element_type=F32
            ).astype(BF16)
        )
    step = column_step(out.shape[1])
    for c in range(0, out.shape[1], step):
        total = jnp.zeros((requests, step), F32)
        for g in range(kv_here):
            total += jnp.dot(
                ordered[g], weight[g, :, c : c + step], preferred_element_type=F32
            )
        out[:, c : c + step] = total.astype(BF16)


def gate(others, *refs):
    residual, gain, here = refs[:3]
    arrived = refs[3 : 3 + others]
    weight, mid_out, left_out, stat_out = refs[3 + others : 7 + others]
    parts = refs[7 + others : -2]
    ordered, squares = refs[-2:]
    blocks, rows, _ = ordered.shape
    width = weight.shape[1]
    mid = residual[...].astype(F32) + here[...].astype(F32)
    for other in arrived:
        mid += other[...].astype(F32)
    mid = mid.astype(BF16).astype(F32)
    share = mid_out.shape[1]
    for j in range(mid_out.shape[0]):
        mid_out[j] = mid[j * share : (j + 1) * share].astype(BF16)
    square = jnp.broadcast_to(jnp.sum(mid * mid, axis=1, keepdims=True), (mid.shape[0], 128))
    scaled = mid * gain[...]
    for k in range(blocks):
        ordered[k] = scaled[k * rows : (k + 1) * rows]
        squares[k] = square[k * rows : (k + 1) * rows]
    mine = lax.axis_index("tok")
    left = jnp.concatenate([ordered[mine ^ k] for k in range(blocks)], axis=0).astype(BF16)
    left_out[...] = left
    lane = lax.broadcasted_iota(jnp.int32, (rows, 128), 1)
    for k in range(blocks):
        value = squares[mine ^ k]
        high = value.astype(BF16).astype(F32)
        middle = (value - high).astype(BF16).astype(F32)
        low = value - high - middle
        stat = jnp.where(lane == 0, high, jnp.where(lane == 1, middle, low))
        stat = jnp.where(lane < 3, stat, 0.0).astype(BF16)
        if k < 2:
            stat_out[k] = stat
        else:
            parts[k][:, width:] = stat
    step = column_step(width)
    for c in range(0, width, step):
        total = jnp.dot(left, weight[:, c : c + step], preferred_element_type=F32)
        for k in range(blocks):
            parts[k][:, c : c + step] = total[k * rows : (k + 1) * rows].astype(BF16)


def up(pieces, left, *refs):
    weights, parts = refs[:pieces], refs[pieces:]
    rows = parts[0].shape[0]
    rhs = left[...]
    base = 0
    for weight in weights:
        width = weight.shape[1]
        step = column_step(width)
        for c in range(0, width, step):
            total = jnp.dot(rhs, weight[:, c : c + step], preferred_element_type=F32)
            at = base + c
            for k, part in enumerate(parts):
                part[:, at : at + step] = total[k * rows : (k + 1) * rows].astype(BF16)
        base += width


def join(up_part, gate_part, stat, *refs):
    out = refs[-1]
    width = up_part.shape[1]
    out[:, :width] = up_part[...]
    out[:, width : 2 * width] = gate_part[...]
    out[:, 2 * width :] = stat[1]


def activate(features, near, *refs):
    out = refs[-1]
    width = out.shape[1]
    own_up, own_gate, own_stat = refs[:3]
    both, refs = refs[3 : 2 + near], refs[2 + near : -1]
    far = len(refs) // 2
    ups, gates = refs[:far], refs[far : 2 * far]
    up_sum = own_up[...].astype(F32)
    gate_sum = own_gate[...].astype(F32)
    stat = own_stat[0].astype(F32)
    for part in both:
        up_sum += part[:, :width].astype(F32)
        gate_sum += part[:, width : 2 * width].astype(F32)
        stat += part[:, 2 * width :].astype(F32)
    for part in ups:
        up_sum += part[...].astype(F32)
    for part in gates:
        gate_sum += part[:, :width].astype(F32)
        stat += part[:, width:].astype(F32)
    square = jnp.sum(stat, axis=1, keepdims=True)
    inv_rms = lax.rsqrt(square / features + 1e-05)
    gated = gate_sum * inv_rms
    out[...] = (gated / (1.0 + jnp.exp(-gated)) * (up_sum * inv_rms)).astype(BF16)


def down(blocks, pieces, *refs):
    parts = refs[:blocks]
    weights = refs[blocks : blocks + pieces]
    outs = refs[blocks + pieces : -1]
    ordered = refs[-1]
    mine, group = lax.axis_index("tok"), lax.axis_index(("ffn", "rep"))
    rows = parts[0].shape[0]
    share = outs[0].shape[0]
    for k in range(blocks):
        at = pl.multiple_of((mine ^ k) * rows, 8)
        ordered[pl.ds(at, rows)] = parts[k][...].astype(F32)
    left = jnp.concatenate(
        [
            ordered[pl.ds(pl.multiple_of((group ^ j) * share, 8), share)]
            for j in range(len(outs))
        ],
        axis=0,
    ).astype(BF16)
    base = 0
    for weight in weights:
        width = weight.shape[1]
        step = column_step(width)
        for c in range(0, width, step):
            total = jnp.dot(left, weight[:, c : c + step], preferred_element_type=F32)
            for j, out in enumerate(outs):
                at = base + c
                out[:, at : at + step] = total[j * share : (j + 1) * share].astype(BF16)
        base += width


def finish(mid, *refs):
    out = refs[-1]
    total = mid[lax.axis_index(("ffn", "rep"))].astype(F32)
    for part in refs[:-1]:
        total += part[...].astype(F32)
    out[...] = total.astype(BF16)


def like(*shape):
    return jax.ShapeDtypeStruct(shape, BF16)


def limit(mib):
    return pltpu.CompilerParams(vmem_limit_bytes=mib * MIB)


def shards(
    queries,
    new_key,
    new_value,
    key_cache,
    value_cache,
    lengths,
    slot_of,
    residual_in,
    out_weight,
    norm_gain,
    gate_weight,
    up_weight,
    down_weight,
):
    tok, ffn, rep = (lax.axis_size(a) for a in ("tok", "ffn", "rep"))
    sums = ffn * rep
    slots, span, kv_width = key_cache.shape
    kv_here = kv_width // HEAD_DIM
    requests, features = residual_in.shape
    hidden_here = gate_weight.shape[1]
    feat_width = out_weight.shape[1]
    in_hbm = functools.partial(pltpu.with_memory_space_constraint, memory_space=pltpu.HBM)

    carried = [
        out_weight,
        slot_of.reshape(1, requests),
        residual_in,
        norm_gain.reshape(1, features),
    ]
    table_rows = slots * kv_here
    *attended, out_weight, slot_of, residual_in, norm_gain = pl.pallas_call(
        functools.partial(attend, ffn),
        out_shape=[like(table_rows, feat_width)] * ffn
        + [pltpu.VMEM(a.shape, a.dtype) for a in carried],
        in_specs=[HBM] * (6 + len(carried)),
        out_specs=[VMEM] * (ffn + len(carried)),
        scratch_shapes=[
            pltpu.SMEM(lengths.shape, jnp.int32),
            pltpu.VMEM(queries.shape, BF16),
            pltpu.VMEM(new_key.shape, BF16),
            pltpu.VMEM(new_value.shape, BF16),
            pltpu.VMEM(key_cache.shape, BF16),
            pltpu.VMEM(value_cache.shape, BF16),
            pltpu.VMEM((ffn, table_rows, feat_width), F32),
            pltpu.SemaphoreType.DMA((4 + 2 * slots + len(carried),)),
        ],
        compiler_params=limit(8),
        cost_estimate=pl.CostEstimate(flops=20000000000, transcendentals=0, bytes_accessed=0),
        name="attend",
    )(
        *(
            in_hbm(a)
            for a in [lengths, queries, new_key, new_value, key_cache, value_cache] + carried
        )
    )
    owners = tok * ffn
    near = min(2, tok)
    close = [attended[0]] + [None] * (near * ffn - 1)
    for k in sorted(range(1, near * ffn), reverse=True):
        close[k] = lax.ppermute(attended[k % ffn], ("tok", "ffn"), swap(owners, k))
    in_vmem = functools.partial(pltpu.with_memory_space_constraint, memory_space=pltpu.VMEM)
    up_pieces = [in_vmem(up_weight)]
    close = pl.pallas_call(
        functools.partial(stack, near * ffn),
        out_shape=like(near * ffn, table_rows, feat_width),
        in_specs=[VMEM] * (near * ffn),
        out_specs=VMEM,
        compiler_params=limit(4),
        name="stack",
    )(*close)
    gathered = [close] + [
        lax.ppermute(close, "tok", swap(tok, k)) for k in range(near, tok, near)
    ]

    partial = pl.pallas_call(
        functools.partial(project, slots),
        out_shape=like(requests, features),
        in_specs=[VMEM] * (2 + len(gathered)),
        out_specs=VMEM,
        compiler_params=limit(8),
        name="project",
    )(slot_of, out_weight, *gathered)
    summed = [partial] + [lax.ppermute(partial, "rep", swap(rep, k)) for k in range(1, rep)]
    here = pl.pallas_call(
        functools.partial(add, len(summed)),
        out_shape=like(requests, features),
        in_specs=[VMEM] * len(summed),
        out_specs=VMEM,
        compiler_params=limit(4),
        name="add",
    )(*summed)
    arrived = [lax.ppermute(here, "ffn", swap(ffn, k)) for k in range(1, ffn)]
    gate_weight = in_vmem(gate_weight)

    rows = requests // tok
    share = requests // sums
    both_width = 2 * hidden_here + 128
    mid, left, stat, *gates = pl.pallas_call(
        functools.partial(gate, len(arrived)),
        out_shape=[like(sums, share, features), like(requests, features), like(near, rows, 128)]
        + [like(rows, hidden_here + (128 if k >= near else 0)) for k in range(tok)],
        in_specs=[VMEM] * (4 + len(arrived)),
        out_specs=[VMEM] * (3 + tok),
        scratch_shapes=[
            pltpu.VMEM((tok, rows, features), F32),
            pltpu.VMEM((tok, rows, 128), F32),
        ],
        compiler_params=limit(8),
        name="gate",
    )(residual_in, norm_gain, here, *arrived, gate_weight)
    far = sorted(range(near, tok), reverse=True)
    got_gates = [lax.ppermute(gates[k], "tok", swap(tok, k)) for k in far]
    ups = pl.pallas_call(
        functools.partial(up, len(up_pieces)),
        out_shape=[like(rows, hidden_here)] * tok,
        in_specs=[VMEM] * (1 + len(up_pieces)),
        out_specs=[VMEM] * tok,
        compiler_params=limit(8),
        cost_estimate=pl.CostEstimate(
            flops=0, transcendentals=0, bytes_accessed=4 * up_weight.size
        ),
        name="up",
    )(left, *up_pieces)
    got_ups = [lax.ppermute(ups[k], "tok", swap(tok, k)) for k in far]
    got_both = []
    if near > 1:
        both = pl.pallas_call(
            join,
            out_shape=like(rows, both_width),
            in_specs=[VMEM] * 3 + [ANY] * len(far),
            out_specs=VMEM,
            compiler_params=limit(4),
            name="join",
        )(ups[1], gates[1], stat, *got_gates)
        got_both.append(lax.ppermute(both, "tok", swap(tok, 1)))

    hidden = pl.pallas_call(
        functools.partial(activate, features * tok, near),
        out_shape=like(rows, hidden_here),
        in_specs=[VMEM] * (2 + near + 2 * len(far)),
        out_specs=VMEM,
        compiler_params=limit(8),
        name="activate",
    )(ups[0], gates[0], stat, *got_both, *got_ups, *got_gates)
    pieces = {k: lax.ppermute(hidden, "tok", swap(tok, k)) for k in sorted(range(1, tok), reverse=True)}

    downs = pl.pallas_call(
        functools.partial(down, tok, 1),
        out_shape=[like(share, features)] * sums,
        in_specs=[VMEM] * (1 + tok),
        out_specs=[VMEM] * sums,
        scratch_shapes=[pltpu.VMEM((requests, hidden_here), F32)],
        compiler_params=limit(8),
        name="down",
    )(hidden, *[pieces[k] for k in range(1, tok)], in_vmem(down_weight))
    order = sorted(range(1, sums), reverse=True)
    got = [downs[0]] + [lax.ppermute(downs[j], ("ffn", "rep"), swap(sums, j)) for j in order]

    return pl.pallas_call(
        finish,
        out_shape=like(share, features),
        in_specs=[VMEM] * (1 + sums),
        out_specs=VMEM,
        compiler_params=limit(8),
        name="finish",
    )(mid, *got)


def solution(mesh):
    placed = (
        P(("groups", "tok", "ffn"), "rep"),
        P(("groups", "tok", "ffn"), "rep"),
        P(("groups", "tok", "ffn"), "rep"),
        P(("groups", "tok", "ffn"), None, "rep"),
        P(("groups", "tok", "ffn"), None, "rep"),
        P(("groups", "tok", "ffn")),
        P("groups"),
        P("groups", "tok"),
        P("rep", "ffn", "tok"),
        P("tok"),
        P("tok", ("ffn", "rep")),
        P("tok", ("ffn", "rep")),
        P(("ffn", "rep"), "tok"),
    )
    return jax.shard_map(
        shards,
        mesh=mesh,
        in_specs=placed,
        out_specs=P(("groups", "ffn", "rep"), "tok"),
        check_vma=False,
    )
```

```python
import functools

import jax
import jax.numpy as jnp
from jax import lax
from jax.experimental import pallas as pl
from jax.experimental.pallas import tpu as pltpu
from jax.sharding import PartitionSpec as P

HEAD_DIM = 128
F32 = jnp.float32
BF16 = jnp.bfloat16
MIB = 2**20
VMEM = pl.BlockSpec(memory_space=pltpu.VMEM)
SMEM = pl.BlockSpec(memory_space=pltpu.SMEM)
ANY = pl.BlockSpec(memory_space=pl.ANY)
HBM = ANY


def swap(extent, step):
    return [(a, a ^ step) for a in range(extent)]


def column_step(width):
    for step in (896, 512, 256, 128):
        if width % step == 0:
            return step
    return width


def attend(peers, lens_in, queries_in, new_key_in, new_value_in, keys, values, *refs):
    count = (len(refs) - 8 - peers) // 2
    carried_in, outs = refs[:count], refs[count : count + peers]
    carried_out = refs[count + peers : 2 * count + peers]
    lens, queries, new_key, new_value, key_buf, value_buf, shares, sems = refs[-8:]
    slots, span, width = key_buf.shape
    kv_here = width // HEAD_DIM
    group = queries.shape[1] // width
    rows = group * slots
    small = [(lens_in, lens), (queries_in, queries), (new_key_in, new_key)]
    small.append((new_value_in, new_value))
    pairs = small + [(keys.at[s], key_buf.at[s]) for s in range(slots)]
    pairs += [(values.at[s], value_buf.at[s]) for s in range(slots)]
    pairs += list(zip(carried_in, carried_out))
    loads = [pltpu.make_async_copy(a, b, sems.at[i]) for i, (a, b) in enumerate(pairs)]
    for load in loads:
        load.start()
    for load in loads[: len(small)]:
        load.wait()
    loads = loads[len(small) :]
    scale = HEAD_DIM ** (-0.5)
    slot_id = lax.rem(lax.broadcasted_iota(jnp.int32, (rows, 1), 0), slots)
    live_len = jnp.zeros((rows, 1), jnp.int32)
    for s in range(slots):
        live_len = jnp.where(slot_id == s, lens[s], live_len)
    live = lax.broadcasted_iota(jnp.int32, (rows, span), 1) < live_len
    q_all = queries[...].astype(F32)
    own_k = new_key[...].astype(F32)
    own_v = new_value[...].astype(F32)
    heads_q, own_score = [], []
    for g in range(kv_here):
        cols = slice(g * HEAD_DIM, (g + 1) * HEAD_DIM)
        first = g * group
        q = jnp.concatenate(
            [
                q_all[:, (first + h) * HEAD_DIM : (first + h + 1) * HEAD_DIM]
                for h in range(group)
            ],
            axis=0,
        )
        k = jnp.concatenate([own_k[:, cols]] * group, axis=0)
        own_score.append(jnp.sum(q * k, axis=1, keepdims=True) * scale)
        heads_q.append(q.astype(BF16))
    scores = [jnp.zeros((rows, span), F32) for _ in range(kv_here)]
    for s in range(slots):
        loads[s].wait()
        for g in range(kv_here):
            here = lax.dot_general(
                heads_q[g],
                key_buf[s, :, g * HEAD_DIM : (g + 1) * HEAD_DIM],
                (((1,), (1,)), ((), ())),
                preferred_element_type=F32,
            )
            scores[g] = jnp.where(slot_id == s, here, scores[g])
    probs, totals = [], []
    for g in range(kv_here):
        masked = jnp.where(live, scores[g] * scale, -jnp.inf)
        top = jnp.maximum(jnp.max(masked, axis=1, keepdims=True), own_score[g])
        exp_cache = jnp.exp(masked - top)
        exp_own = jnp.exp(own_score[g] - top)
        total = jnp.sum(exp_cache, axis=1, keepdims=True) + exp_own
        probs.append((exp_cache / total).astype(BF16))
        own = jnp.concatenate(
            [own_v[:, g * HEAD_DIM : (g + 1) * HEAD_DIM]] * group, axis=0
        )
        totals.append((exp_own / total).astype(BF16).astype(F32) * own)
    for s in range(slots):
        loads[slots + s].wait()
        for g in range(kv_here):
            here = jnp.where(slot_id == s, probs[g], jnp.zeros_like(probs[g]))
            totals[g] += jnp.dot(
                here,
                value_buf[s, :, g * HEAD_DIM : (g + 1) * HEAD_DIM],
                preferred_element_type=F32,
            )
    heads_out = group // peers
    for f in range(peers):
        shares[f] = jnp.concatenate(
            [
                jnp.concatenate(
                    [totals[g][h * slots : (h + 1) * slots] for g in range(kv_here)], axis=0
                )
                for h in range(f * heads_out, (f + 1) * heads_out)
            ],
            axis=1,
        )
    mine = lax.axis_index("ffn")
    for f in range(peers):
        outs[f][...] = shares[mine ^ f].astype(BF16)
    for load in loads[2 * slots :]:
        load.wait()


def stack(count, *refs):
    out = refs[-1]
    for i, ref in enumerate(refs[:count]):
        out[i] = ref[...]


def add(count, *refs):
    total = refs[0][...].astype(F32)
    for ref in refs[1:count]:
        total += ref[...].astype(F32)
    refs[-1][...] = total.astype(BF16)


def project(slots, slot_of, weight, *refs):
    refs, out = refs[:-1], refs[-1]
    requests = slot_of.shape[1]
    _, rows, width = refs[0].shape
    kv_here = weight.shape[0]
    table = [ref[...].astype(F32).reshape(ref.shape[0] * rows, width) for ref in refs]
    table = jnp.concatenate(table, axis=0).astype(BF16)
    slot = slot_of[...]
    mine = lax.axis_index(("tok", "ffn"))
    where_from = ((slot // slots) ^ mine) * rows + lax.rem(slot, slots)
    row = lax.broadcasted_iota(jnp.int32, (table.shape[0], requests), 0)
    ordered = []
    for g in range(kv_here):
        pick = (row == where_from + g * slots).astype(F32).astype(BF16)
        ordered.append(
            lax.dot_general(
                pick, table, (((0,), (0,)), ((), ())), preferred_element_type=F32
            ).astype(BF16)
        )
    step = column_step(out.shape[1])
    for c in range(0, out.shape[1], step):
        total = jnp.zeros((requests, step), F32)
        for g in range(kv_here):
            total += jnp.dot(
                ordered[g], weight[g, :, c : c + step], preferred_element_type=F32
            )
        out[:, c : c + step] = total.astype(BF16)


def gate(others, *refs):
    residual, gain, here = refs[:3]
    arrived = refs[3 : 3 + others]
    weight, mid_out, left_out, stat_out, out = refs[3 + others : 8 + others]
    ordered, squares = refs[-2:]
    blocks, rows, _ = ordered.shape
    width = weight.shape[1]
    mid = residual[...].astype(F32) + here[...].astype(F32)
    for other in arrived:
        mid += other[...].astype(F32)
    mid = mid.astype(BF16).astype(F32)
    share = mid_out.shape[1]
    for j in range(mid_out.shape[0]):
        mid_out[j] = mid[j * share : (j + 1) * share].astype(BF16)
    square = jnp.broadcast_to(jnp.sum(mid * mid, axis=1, keepdims=True), (mid.shape[0], 128))
    scaled = mid * gain[...]
    for k in range(blocks):
        ordered[k] = scaled[k * rows : (k + 1) * rows]
        squares[k] = square[k * rows : (k + 1) * rows]
    mine = lax.axis_index("tok")
    left = jnp.concatenate([ordered[mine ^ k] for k in range(blocks)], axis=0).astype(BF16)
    left_out[...] = left
    lane = lax.broadcasted_iota(jnp.int32, (rows, 128), 1)
    for k in range(blocks):
        value = squares[mine ^ k]
        high = value.astype(BF16).astype(F32)
        middle = (value - high).astype(BF16).astype(F32)
        low = value - high - middle
        stat = jnp.where(lane == 0, high, jnp.where(lane == 1, middle, low))
        stat_out[k] = jnp.where(lane < 3, stat, 0.0).astype(BF16)
    step = column_step(width)
    for c in range(0, width, step):
        total = jnp.dot(left, weight[:, c : c + step], preferred_element_type=F32)
        for k in range(blocks):
            out[k, :, c : c + step] = total[k * rows : (k + 1) * rows].astype(BF16)


def up(left, stat, gates, weight, *parts):
    rows = parts[0].shape[0]
    width = weight.shape[1]
    for k, part in enumerate(parts):
        part[:, :width] = gates[k]
        part[:, 2 * width :] = stat[k]
    rhs = left[...]
    step = column_step(width)
    for c in range(0, width, step):
        total = jnp.dot(rhs, weight[:, c : c + step], preferred_element_type=F32)
        for k, part in enumerate(parts):
            part[:, width + c : width + c + step] = total[k * rows : (k + 1) * rows].astype(BF16)


def activate(features, *refs):
    out = refs[-1]
    width = out.shape[1]
    total = refs[0][...].astype(F32)
    for part in refs[1:-1]:
        total += part[...].astype(F32)
    square = jnp.sum(total[:, 2 * width :], axis=1, keepdims=True)
    inv_rms = lax.rsqrt(square / features + 1e-05)
    gate = total[:, :width] * inv_rms
    up = total[:, width : 2 * width] * inv_rms
    out[...] = (gate / (1.0 + jnp.exp(-gate)) * up).astype(BF16)


def down(blocks, pieces, *refs):
    parts = refs[:blocks]
    weights = refs[blocks : blocks + pieces]
    outs = refs[blocks + pieces : -1]
    ordered = refs[-1]
    mine, group = lax.axis_index("tok"), lax.axis_index(("ffn", "rep"))
    rows = parts[0].shape[0]
    share = outs[0].shape[0]
    for k in range(blocks):
        at = pl.multiple_of((mine ^ k) * rows, 8)
        ordered[pl.ds(at, rows)] = parts[k][...].astype(F32)
    left = jnp.concatenate(
        [
            ordered[pl.ds(pl.multiple_of((group ^ j) * share, 8), share)]
            for j in range(len(outs))
        ],
        axis=0,
    ).astype(BF16)
    base = 0
    for weight in weights:
        width = weight.shape[1]
        step = column_step(width)
        for c in range(0, width, step):
            total = jnp.dot(left, weight[:, c : c + step], preferred_element_type=F32)
            for j, out in enumerate(outs):
                at = base + c
                out[:, at : at + step] = total[j * share : (j + 1) * share].astype(BF16)
        base += width


def finish(mid, *refs):
    out = refs[-1]
    total = mid[lax.axis_index(("ffn", "rep"))].astype(F32)
    for part in refs[:-1]:
        total += part[...].astype(F32)
    out[...] = total.astype(BF16)


def like(*shape):
    return jax.ShapeDtypeStruct(shape, BF16)


def limit(mib):
    return pltpu.CompilerParams(vmem_limit_bytes=mib * MIB)


def shards(
    queries,
    new_key,
    new_value,
    key_cache,
    value_cache,
    lengths,
    slot_of,
    residual_in,
    out_weight,
    norm_gain,
    gate_weight,
    up_weight,
    down_weight,
):
    tok, ffn, rep = (lax.axis_size(a) for a in ("tok", "ffn", "rep"))
    sums = ffn * rep
    slots, span, kv_width = key_cache.shape
    kv_here = kv_width // HEAD_DIM
    requests, features = residual_in.shape
    hidden_here = gate_weight.shape[1]
    feat_width = out_weight.shape[1]
    in_hbm = functools.partial(pltpu.with_memory_space_constraint, memory_space=pltpu.HBM)

    carried = [
        slot_of.reshape(1, requests),
        residual_in,
        norm_gain.reshape(1, features),
    ]
    table_rows = slots * kv_here
    *attended, slot_of, residual_in, norm_gain = pl.pallas_call(
        functools.partial(attend, ffn),
        out_shape=[like(table_rows, feat_width)] * ffn
        + [pltpu.VMEM(a.shape, a.dtype) for a in carried],
        in_specs=[HBM] * (6 + len(carried)),
        out_specs=[VMEM] * (ffn + len(carried)),
        scratch_shapes=[
            pltpu.SMEM(lengths.shape, jnp.int32),
            pltpu.VMEM(queries.shape, BF16),
            pltpu.VMEM(new_key.shape, BF16),
            pltpu.VMEM(new_value.shape, BF16),
            pltpu.VMEM(key_cache.shape, BF16),
            pltpu.VMEM(value_cache.shape, BF16),
            pltpu.VMEM((ffn, table_rows, feat_width), F32),
            pltpu.SemaphoreType.DMA((4 + 2 * slots + len(carried),)),
        ],
        compiler_params=limit(3),
        cost_estimate=pl.CostEstimate(flops=20000000000, transcendentals=0, bytes_accessed=0),
        name="attend",
    )(
        *(
            in_hbm(a)
            for a in [lengths, queries, new_key, new_value, key_cache, value_cache] + carried
        )
    )
    owners = tok * ffn
    near = min(2, tok)
    out_weight = pltpu.with_memory_space_constraint(out_weight, pltpu.VMEM)
    in_vmem = functools.partial(pltpu.with_memory_space_constraint, memory_space=pltpu.VMEM)
    close = [None] * (near * ffn)
    for k in reversed(range(near * ffn)):
        close[k] = lax.ppermute(
            attended[k % ffn], ("tok", "ffn", "rep"), swap(owners * rep, k * rep + rep - 1)
        )
    close = pl.pallas_call(
        functools.partial(stack, near * ffn),
        out_shape=like(near * ffn, table_rows, feat_width),
        in_specs=[VMEM] * (near * ffn),
        out_specs=VMEM,
        compiler_params=limit(3),
        name="stack",
    )(*close)
    gathered = [
        lax.ppermute(close, ("tok", "rep"), swap(tok * rep, k * rep + rep - 1))
        for k in range(0, tok, near)
    ]

    partial = pl.pallas_call(
        functools.partial(project, slots),
        out_shape=like(requests, features),
        in_specs=[VMEM] * (2 + len(gathered)),
        out_specs=VMEM,
        compiler_params=limit(3),
        name="project",
    )(slot_of, out_weight, *gathered)
    summed = [partial] + [lax.ppermute(partial, "rep", swap(rep, k)) for k in range(1, rep)]
    here = pl.pallas_call(
        functools.partial(add, len(summed)),
        out_shape=like(requests, features),
        in_specs=[VMEM] * len(summed),
        out_specs=VMEM,
        compiler_params=limit(3),
        name="add",
    )(*summed)
    arrived = [lax.ppermute(here, "ffn", swap(ffn, k)) for k in range(1, ffn)]
    gate_weight = in_vmem(gate_weight)

    rows = requests // tok
    share = requests // sums
    mid, left, stat, gates = pl.pallas_call(
        functools.partial(gate, len(arrived)),
        out_shape=[
            like(sums, share, features),
            like(requests, features),
            like(tok, rows, 128),
            like(tok, rows, hidden_here),
        ],
        in_specs=[VMEM] * (4 + len(arrived)),
        out_specs=[VMEM] * 4,
        scratch_shapes=[
            pltpu.VMEM((tok, rows, features), F32),
            pltpu.VMEM((tok, rows, 128), F32),
        ],
        compiler_params=limit(3),
        name="gate",
    )(residual_in, norm_gain, here, *arrived, gate_weight)
    parts = pl.pallas_call(
        up,
        out_shape=[like(rows, 2 * hidden_here + 128)] * tok,
        in_specs=[VMEM] * 4,
        out_specs=[VMEM] * tok,
        compiler_params=limit(3),
        name="up",
    )(left, stat, gates, in_vmem(up_weight))
    order = sorted(range(1, tok), reverse=True)
    got = [parts[0]] + [lax.ppermute(parts[k], "tok", swap(tok, k)) for k in order]

    hidden = pl.pallas_call(
        functools.partial(activate, features * tok),
        out_shape=like(rows, hidden_here),
        in_specs=[VMEM] * tok,
        out_specs=VMEM,
        compiler_params=limit(3),
        name="activate",
    )(*got)
    pieces = {k: lax.ppermute(hidden, "tok", swap(tok, k)) for k in sorted(range(1, tok), reverse=True)}

    downs = pl.pallas_call(
        functools.partial(down, tok, 1),
        out_shape=[like(share, features)] * sums,
        in_specs=[VMEM] * (1 + tok),
        out_specs=[VMEM] * sums,
        scratch_shapes=[pltpu.VMEM((requests, hidden_here), F32)],
        compiler_params=limit(3),
        name="down",
    )(hidden, *[pieces[k] for k in range(1, tok)], in_vmem(down_weight))
    order = sorted(range(1, sums), reverse=True)
    got = [downs[0]] + [lax.ppermute(downs[j], ("ffn", "rep"), swap(sums, j)) for j in order]

    return pl.pallas_call(
        finish,
        out_shape=like(share, features),
        in_specs=[VMEM] * (1 + sums),
        out_specs=VMEM,
        compiler_params=limit(3),
        name="finish",
    )(mid, *got)


def solution(mesh):
    placed = (
        P(("groups", "tok", "ffn"), "rep"),
        P(("groups", "tok", "ffn"), "rep"),
        P(("groups", "tok", "ffn"), "rep"),
        P(("groups", "tok", "ffn"), None, "rep"),
        P(("groups", "tok", "ffn"), None, "rep"),
        P(("groups", "tok", "ffn")),
        P("groups"),
        P("groups", "tok"),
        P("rep", "ffn", "tok"),
        P("tok"),
        P("tok", ("ffn", "rep")),
        P("tok", ("ffn", "rep")),
        P(("ffn", "rep"), "tok"),
    )
    return jax.shard_map(
        shards,
        mesh=mesh,
        in_specs=placed,
        out_specs=P(("groups", "ffn", "rep"), "tok"),
        check_vma=False,
    )
```

```python
import functools

import jax
import jax.numpy as jnp
from jax import lax
from jax.experimental import pallas as pl
from jax.experimental.pallas import tpu as pltpu
from jax.sharding import PartitionSpec as P

HEAD_DIM = 128
F32 = jnp.float32
BF16 = jnp.bfloat16
MIB = 2**20
VMEM = pl.BlockSpec(memory_space=pltpu.VMEM)
SMEM = pl.BlockSpec(memory_space=pltpu.SMEM)
ANY = pl.BlockSpec(memory_space=pl.ANY)
HBM = ANY


def swap(extent, step):
    return [(a, a ^ step) for a in range(extent)]


def column_step(width):
    for step in (896, 512, 256, 128):
        if width % step == 0:
            return step
    return width


def attend(peers, lens_in, queries_in, new_key_in, new_value_in, keys, values, *refs):
    count = (len(refs) - 8 - peers) // 2
    carried_in, outs = refs[:count], refs[count : count + peers]
    carried_out = refs[count + peers : 2 * count + peers]
    lens, queries, new_key, new_value, key_buf, value_buf, shares, sems = refs[-8:]
    slots, span, width = key_buf.shape
    kv_here = width // HEAD_DIM
    group = queries.shape[1] // width
    rows = group * slots
    small = [(lens_in, lens), (queries_in, queries), (new_key_in, new_key)]
    small.append((new_value_in, new_value))
    pairs = small + [(keys.at[s], key_buf.at[s]) for s in range(slots)]
    pairs += [(values.at[s], value_buf.at[s]) for s in range(slots)]
    for a, b in zip(carried_in, carried_out):
        if a.shape == b.shape:
            pairs.append((a, b))
        else:
            part = b.shape[2]
            pairs += [(a.at[:, pl.ds(p * part, part)], b.at[p]) for p in range(b.shape[0])]
    loads = [pltpu.make_async_copy(a, b, sems.at[i]) for i, (a, b) in enumerate(pairs)]
    for load in loads:
        load.start()
    for load in loads[: len(small)]:
        load.wait()
    loads = loads[len(small) :]
    scale = HEAD_DIM ** (-0.5)
    slot_id = lax.rem(lax.broadcasted_iota(jnp.int32, (rows, 1), 0), slots)
    live_len = jnp.zeros((rows, 1), jnp.int32)
    for s in range(slots):
        live_len = jnp.where(slot_id == s, lens[s], live_len)
    live = lax.broadcasted_iota(jnp.int32, (rows, span), 1) < live_len
    q_all = queries[...].astype(F32)
    own_k = new_key[...].astype(F32)
    own_v = new_value[...].astype(F32)
    heads_q, own_score = [], []
    for g in range(kv_here):
        cols = slice(g * HEAD_DIM, (g + 1) * HEAD_DIM)
        first = g * group
        q = jnp.concatenate(
            [
                q_all[:, (first + h) * HEAD_DIM : (first + h + 1) * HEAD_DIM]
                for h in range(group)
            ],
            axis=0,
        )
        k = jnp.concatenate([own_k[:, cols]] * group, axis=0)
        own_score.append(jnp.sum(q * k, axis=1, keepdims=True) * scale)
        heads_q.append(q.astype(BF16))
    scores = [jnp.zeros((rows, span), F32) for _ in range(kv_here)]
    for s in range(slots):
        loads[s].wait()
        for g in range(kv_here):
            here = lax.dot_general(
                heads_q[g],
                key_buf[s, :, g * HEAD_DIM : (g + 1) * HEAD_DIM],
                (((1,), (1,)), ((), ())),
                preferred_element_type=F32,
            )
            scores[g] = jnp.where(slot_id == s, here, scores[g])
    probs, totals = [], []
    for g in range(kv_here):
        masked = jnp.where(live, scores[g] * scale, -jnp.inf)
        top = jnp.maximum(jnp.max(masked, axis=1, keepdims=True), own_score[g])
        exp_cache = jnp.exp(masked - top)
        exp_own = jnp.exp(own_score[g] - top)
        total = jnp.sum(exp_cache, axis=1, keepdims=True) + exp_own
        probs.append((exp_cache / total).astype(BF16))
        own = jnp.concatenate(
            [own_v[:, g * HEAD_DIM : (g + 1) * HEAD_DIM]] * group, axis=0
        )
        totals.append((exp_own / total).astype(BF16).astype(F32) * own)
    for s in range(slots):
        loads[slots + s].wait()
        for g in range(kv_here):
            here = jnp.where(slot_id == s, probs[g], jnp.zeros_like(probs[g]))
            totals[g] += jnp.dot(
                here,
                value_buf[s, :, g * HEAD_DIM : (g + 1) * HEAD_DIM],
                preferred_element_type=F32,
            )
    heads_out = group // peers
    for f in range(peers):
        shares[f] = jnp.concatenate(
            [
                jnp.concatenate(
                    [totals[g][h * slots : (h + 1) * slots] for g in range(kv_here)], axis=0
                )
                for h in range(f * heads_out, (f + 1) * heads_out)
            ],
            axis=1,
        )
    mine = lax.axis_index("ffn")
    for f in range(peers):
        outs[f][...] = shares[mine ^ f].astype(BF16)
    for load in loads[2 * slots :]:
        load.wait()


def stack(count, *refs):
    out = refs[-1]
    for i, ref in enumerate(refs[:count]):
        out[i] = ref[...]


def add(count, *refs):
    total = refs[0][...].astype(F32)
    for ref in refs[1:count]:
        total += ref[...].astype(F32)
    refs[-1][...] = total.astype(BF16)


def project(slots, peers, slot_of, weight, *refs):
    refs, outs, parts = refs[: -1 - peers], refs[-1 - peers : -1], refs[-1]
    requests = slot_of.shape[1]
    _, rows, width = refs[0].shape
    kv_here = weight.shape[0]
    table = [ref[...].astype(F32).reshape(ref.shape[0] * rows, width) for ref in refs]
    table = jnp.concatenate(table, axis=0).astype(BF16)
    slot = slot_of[...]
    mine = lax.axis_index(("tok", "ffn"))
    where_from = ((slot // slots) ^ mine) * rows + lax.rem(slot, slots)
    row = lax.broadcasted_iota(jnp.int32, (table.shape[0], requests), 0)
    ordered = []
    for g in range(kv_here):
        pick = (row == where_from + g * slots).astype(F32).astype(BF16)
        ordered.append(
            lax.dot_general(
                pick, table, (((0,), (0,)), ((), ())), preferred_element_type=F32
            ).astype(BF16)
        )
    width = parts.shape[2]
    step = column_step(width)
    for p in range(peers):
        for c in range(0, width, step):
            at = p * width + c
            total = jnp.zeros((requests, step), F32)
            for g in range(kv_here):
                total += jnp.dot(
                    ordered[g], weight[g, :, at : at + step], preferred_element_type=F32
                )
            parts[p, :, c : c + step] = total
    core = lax.axis_index("rep")
    for p, out in enumerate(outs):
        out[...] = parts[core ^ p].astype(BF16)


def by_owner(value, ordered):
    blocks, rows, _ = ordered.shape
    mine = lax.axis_index("tok")
    for k in range(blocks):
        ordered[k] = value[k * rows : (k + 1) * rows]
    return jnp.concatenate([ordered[mine ^ k] for k in range(blocks)], axis=0)


def part_rows(peer, height):
    return pl.ds(pl.multiple_of((lax.axis_index("rep") ^ peer) * height, height), height)


def own_part(core, mid, gain, weight, left, sums, ordered):
    @pl.when(lax.axis_index("rep") == core)
    def _():
        scaled = mid[...].astype(F32) * gain[core]
        rhs = by_owner(scaled, ordered).astype(BF16)
        left[...] = rhs
        height = mid.shape[1]
        step = column_step(weight.shape[1])
        for c in range(0, weight.shape[1], step):
            sums[:, c : c + step] = jnp.dot(
                rhs,
                weight[core * height : (core + 1) * height, c : c + step],
                preferred_element_type=F32,
            )


def gate_first(core, residual, gain, weight, *refs):
    mid, left, sums, ordered = refs[-4:]
    total = residual[lax.axis_index("rep")].astype(F32)
    for ref in refs[:-4]:
        total += ref[...].astype(F32)
    mid[...] = total.astype(BF16)
    own_part(core, mid, gain, weight, left, sums, ordered)


def gate_next(core, mid, gain, weight, left_in, sums_in, left, sums, ordered):
    own_part(core, mid, gain, weight, left, sums, ordered)


def up_own(left, weight, sums):
    rhs = left[...]
    at = part_rows(0, left.shape[1])
    step = column_step(weight.shape[1])
    for c in range(0, weight.shape[1], step):
        sums[:, c : c + step] = jnp.dot(
            rhs, weight[at, c : c + step], preferred_element_type=F32
        )


def gate_rest(peers, *refs):
    mids = refs[:peers]
    gain, weight, sums, mid_out, left, stat_out, out, ordered, squares = refs[peers:]
    blocks, rows, height = ordered.shape
    core = lax.axis_index("rep")
    share = mid_out.shape[2]
    square = jnp.zeros((blocks * rows, 1), F32)
    lefts = []
    for p in range(peers):
        mid = mids[p][...].astype(F32)
        for j in range(mid_out.shape[1]):
            mid_out[core ^ p, j] = mid[j * share : (j + 1) * share].astype(BF16)
        square += jnp.sum(mid * mid, axis=1, keepdims=True)
        if p > 0:
            scaled = by_owner(mid * gain[core ^ p], ordered).astype(BF16)
            left[p - 1] = scaled
            lefts.append(scaled)
    square = by_owner(jnp.broadcast_to(square, (blocks * rows, 128)), squares)
    high = square.astype(BF16).astype(F32)
    medium = (square - high).astype(BF16).astype(F32)
    low = square - high - medium
    lane = lax.broadcasted_iota(jnp.int32, square.shape, 1)
    stat = jnp.where(lane == 0, high, jnp.where(lane == 1, medium, low))
    stat = jnp.where(lane < 3, stat, 0.0).astype(BF16)
    for k in range(blocks):
        stat_out[k] = stat[k * rows : (k + 1) * rows]
    width = weight.shape[1]
    step = column_step(width)
    for c in range(0, width, step):
        total = sums[:, c : c + step]
        for p in range(1, peers):
            total += jnp.dot(
                lefts[p - 1],
                weight[part_rows(p, height), c : c + step],
                preferred_element_type=F32,
            )
        for k in range(blocks):
            out[k, :, c : c + step] = total[k * rows : (k + 1) * rows].astype(BF16)


def up_rest(sums, rest, stat, gates, weight, *parts):
    rows = parts[0].shape[0]
    height, width = rest.shape[2], weight.shape[1]
    for k, part in enumerate(parts):
        part[:, :width] = gates[k]
        part[:, 2 * width :] = stat[k]
    lefts = [rest[p] for p in range(rest.shape[0])]
    step = column_step(width)
    for c in range(0, width, step):
        total = sums[:, c : c + step]
        for p, left in enumerate(lefts):
            total += jnp.dot(
                left, weight[part_rows(p + 1, height), c : c + step], preferred_element_type=F32
            )
        for k, part in enumerate(parts):
            part[:, width + c : width + c + step] = total[k * rows : (k + 1) * rows].astype(BF16)


def activate(features, *refs):
    out = refs[-1]
    width = out.shape[1]
    total = refs[0][...].astype(F32)
    for part in refs[1:-1]:
        total += part[...].astype(F32)
    square = jnp.sum(total[:, 2 * width :], axis=1, keepdims=True)
    inv_rms = lax.rsqrt(square / features + 1e-05)
    gate = total[:, :width] * inv_rms
    up = total[:, width : 2 * width] * inv_rms
    out[...] = (gate / (1.0 + jnp.exp(-gate)) * up).astype(BF16)


def down(blocks, pieces, *refs):
    parts = refs[:blocks]
    weights = refs[blocks : blocks + pieces]
    outs = refs[blocks + pieces : -1]
    ordered = refs[-1]
    mine, group = lax.axis_index("tok"), lax.axis_index(("ffn", "rep"))
    rows = parts[0].shape[0]
    share = outs[0].shape[0]
    for k in range(blocks):
        at = pl.multiple_of((mine ^ k) * rows, 8)
        ordered[pl.ds(at, rows)] = parts[k][...].astype(F32)
    left = jnp.concatenate(
        [
            ordered[pl.ds(pl.multiple_of((group ^ j) * share, 8), share)]
            for j in range(len(outs))
        ],
        axis=0,
    ).astype(BF16)
    base = 0
    for weight in weights:
        width = weight.shape[1]
        step = column_step(width)
        for c in range(0, width, step):
            total = jnp.dot(left, weight[:, c : c + step], preferred_element_type=F32)
            for j, out in enumerate(outs):
                at = base + c
                out[:, at : at + step] = total[j * share : (j + 1) * share].astype(BF16)
        base += width


def finish(mid, *refs):
    mine = lax.axis_index(("ffn", "rep"))
    out = refs[-1]
    total = jnp.concatenate([mid[p, mine] for p in range(mid.shape[0])], axis=1).astype(F32)
    for part in refs[:-1]:
        total += part[...].astype(F32)
    out[...] = total.astype(BF16)


def like(*shape):
    return jax.ShapeDtypeStruct(shape, BF16)


def limit(mib):
    return pltpu.CompilerParams(vmem_limit_bytes=mib * MIB)


def shards(
    queries,
    new_key,
    new_value,
    key_cache,
    value_cache,
    lengths,
    slot_of,
    residual_in,
    out_weight,
    norm_gain,
    gate_weight,
    up_weight,
    down_weight,
):
    tok, ffn, rep = (lax.axis_size(a) for a in ("tok", "ffn", "rep"))
    sums = ffn * rep
    slots, span, kv_width = key_cache.shape
    kv_here = kv_width // HEAD_DIM
    requests, features = residual_in.shape
    hidden_here = gate_weight.shape[1]
    feat_width = out_weight.shape[1]
    in_hbm = functools.partial(pltpu.with_memory_space_constraint, memory_space=pltpu.HBM)

    height = features // rep
    slot_of = slot_of.reshape(1, requests)
    carried = [
        slot_of,
        residual_in,
        norm_gain.reshape(1, features),
    ]
    table_rows = slots * kv_here
    *attended, slot_of, residual_in, norm_gain = pl.pallas_call(
        functools.partial(attend, ffn),
        out_shape=[like(table_rows, feat_width)] * ffn
        + [
            pltpu.VMEM(slot_of.shape, slot_of.dtype),
            pltpu.VMEM((rep, requests, height), BF16),
            pltpu.VMEM((rep, 1, height), F32),
        ],
        in_specs=[HBM] * (6 + len(carried)),
        out_specs=[VMEM] * (ffn + len(carried)),
        scratch_shapes=[
            pltpu.SMEM(lengths.shape, jnp.int32),
            pltpu.VMEM(queries.shape, BF16),
            pltpu.VMEM(new_key.shape, BF16),
            pltpu.VMEM(new_value.shape, BF16),
            pltpu.VMEM(key_cache.shape, BF16),
            pltpu.VMEM(value_cache.shape, BF16),
            pltpu.VMEM((ffn, table_rows, feat_width), F32),
            pltpu.SemaphoreType.DMA((5 + 2 * slots + 2 * rep,)),
        ],
        compiler_params=limit(3),
        cost_estimate=pl.CostEstimate(flops=20000000000, transcendentals=0, bytes_accessed=0),
        name="attend",
    )(
        *(
            in_hbm(a)
            for a in [lengths, queries, new_key, new_value, key_cache, value_cache] + carried
        )
    )
    owners = tok * ffn
    near = min(2, tok)
    out_weight = pltpu.with_memory_space_constraint(out_weight, pltpu.VMEM)
    in_vmem = functools.partial(pltpu.with_memory_space_constraint, memory_space=pltpu.VMEM)
    close = [None] * (near * ffn)
    for k in reversed(range(near * ffn)):
        close[k] = lax.ppermute(
            attended[k % ffn], ("tok", "ffn", "rep"), swap(owners * rep, k * rep + rep - 1)
        )
    close = pl.pallas_call(
        functools.partial(stack, near * ffn),
        out_shape=like(near * ffn, table_rows, feat_width),
        in_specs=[VMEM] * (near * ffn),
        out_specs=VMEM,
        compiler_params=limit(3),
        name="stack",
    )(*close)
    gathered = [
        lax.ppermute(close, ("tok", "rep"), swap(tok * rep, k * rep + rep - 1))
        for k in range(0, tok, near)
    ]

    partials = pl.pallas_call(
        functools.partial(project, slots, rep),
        out_shape=[like(requests, height)] * rep,
        in_specs=[VMEM] * (2 + len(gathered)),
        out_specs=[VMEM] * rep,
        scratch_shapes=[pltpu.VMEM((rep, requests, height), F32)],
        compiler_params=limit(3),
        cost_estimate=pl.CostEstimate(flops=10000000000, transcendentals=0, bytes_accessed=0),
        name="project",
    )(slot_of, out_weight, *gathered)
    summed = [partials[0]] + [
        lax.ppermute(partials[k], "rep", swap(rep, k)) for k in range(1, rep)
    ]
    up_weight = in_vmem(up_weight)
    here = pl.pallas_call(
        functools.partial(add, len(summed)),
        out_shape=like(requests, height),
        in_specs=[VMEM] * (len(summed) + 1),
        out_specs=VMEM,
        compiler_params=limit(3),
        name="add",
    )(*summed, up_weight)
    arrived = [lax.ppermute(here, "ffn", swap(ffn, k)) for k in range(1, ffn)]
    gate_weight = in_vmem(gate_weight)
    rows = requests // tok
    share = requests // sums
    own_shapes = [like(requests, height), jax.ShapeDtypeStruct((requests, hidden_here), F32)]
    mid_own, own, own_sums = pl.pallas_call(
        functools.partial(gate_first, rep - 1),
        out_shape=[like(requests, height)] + own_shapes,
        in_specs=[VMEM] * (3 + ffn),
        out_specs=[VMEM] * 3,
        scratch_shapes=[pltpu.VMEM((tok, rows, height), F32)],
        compiler_params=limit(3),
        name="gate_first",
    )(residual_in, norm_gain, gate_weight, here, *arrived)
    mids = [mid_own] + [lax.ppermute(mid_own, "rep", swap(rep, k)) for k in range(1, rep)]
    for core in reversed(range(rep - 1)):
        own, own_sums = pl.pallas_call(
            functools.partial(gate_next, core),
            out_shape=own_shapes,
            in_specs=[VMEM] * 5,
            out_specs=[VMEM] * 2,
            input_output_aliases={3: 0, 4: 1},
            scratch_shapes=[pltpu.VMEM((tok, rows, height), F32)],
            compiler_params=limit(3),
            name="gate_next",
        )(mid_own, norm_gain, gate_weight, own, own_sums)
    up_sums = pl.pallas_call(
        up_own,
        out_shape=own_shapes[1],
        in_specs=[VMEM] * 2,
        out_specs=VMEM,
        compiler_params=limit(3),
        name="up_own",
    )(own, up_weight)
    mid, rest, stat, gates = pl.pallas_call(
        functools.partial(gate_rest, rep),
        out_shape=[
            like(rep, sums, share, height),
            like(rep - 1, requests, height),
            like(tok, rows, 128),
            like(tok, rows, hidden_here),
        ],
        in_specs=[VMEM] * (3 + rep),
        out_specs=[VMEM] * 4,
        scratch_shapes=[
            pltpu.VMEM((tok, rows, height), F32),
            pltpu.VMEM((tok, rows, 128), F32),
        ],
        compiler_params=limit(3),
        name="gate_rest",
    )(*mids, norm_gain, gate_weight, own_sums)
    parts = pl.pallas_call(
        up_rest,
        out_shape=[like(rows, 2 * hidden_here + 128)] * tok,
        in_specs=[VMEM] * 5,
        out_specs=[VMEM] * tok,
        compiler_params=limit(3),
        name="up_rest",
    )(up_sums, rest, stat, gates, up_weight)
    order = sorted(range(1, tok), reverse=True)
    got = [parts[0]] + [lax.ppermute(parts[k], "tok", swap(tok, k)) for k in order]

    hidden = pl.pallas_call(
        functools.partial(activate, features * tok),
        out_shape=like(rows, hidden_here),
        in_specs=[VMEM] * tok,
        out_specs=VMEM,
        compiler_params=limit(3),
        name="activate",
    )(*got)
    pieces = {k: lax.ppermute(hidden, "tok", swap(tok, k)) for k in sorted(range(1, tok), reverse=True)}

    downs = pl.pallas_call(
        functools.partial(down, tok, 1),
        out_shape=[like(share, features)] * sums,
        in_specs=[VMEM] * (1 + tok),
        out_specs=[VMEM] * sums,
        scratch_shapes=[pltpu.VMEM((requests, hidden_here), F32)],
        compiler_params=limit(3),
        name="down",
    )(hidden, *[pieces[k] for k in range(1, tok)], in_vmem(down_weight))
    order = sorted(range(1, sums), reverse=True)
    got = [downs[0]] + [lax.ppermute(downs[j], ("ffn", "rep"), swap(sums, j)) for j in order]

    return pl.pallas_call(
        finish,
        out_shape=like(share, features),
        in_specs=[VMEM] * (1 + sums),
        out_specs=VMEM,
        compiler_params=limit(3),
        name="finish",
    )(mid, *got)


def solution(mesh):
    placed = (
        P(("groups", "tok", "ffn"), "rep"),
        P(("groups", "tok", "ffn"), "rep"),
        P(("groups", "tok", "ffn"), "rep"),
        P(("groups", "tok", "ffn"), None, "rep"),
        P(("groups", "tok", "ffn"), None, "rep"),
        P(("groups", "tok", "ffn")),
        P("groups"),
        P("groups", "tok"),
        P("rep", "ffn", "tok"),
        P("tok"),
        P("tok", ("ffn", "rep")),
        P("tok", ("ffn", "rep")),
        P(("ffn", "rep"), "tok"),
    )
    return jax.shard_map(
        shards,
        mesh=mesh,
        in_specs=placed,
        out_specs=P(("groups", "ffn", "rep"), "tok"),
        check_vma=False,
    )
```

```python
import functools

import jax
import jax.numpy as jnp
from jax import lax
from jax.experimental import pallas as pl
from jax.experimental.pallas import tpu as pltpu
from jax.sharding import PartitionSpec as P

HEAD_DIM = 128
F32 = jnp.float32
BF16 = jnp.bfloat16
MIB = 2**20
VMEM = pl.BlockSpec(memory_space=pltpu.VMEM)
SMEM = pl.BlockSpec(memory_space=pltpu.SMEM)
ANY = pl.BlockSpec(memory_space=pl.ANY)
HBM = ANY


def swap(extent, step):
    return [(a, a ^ step) for a in range(extent)]


def column_step(width):
    for step in (896, 512, 256, 128):
        if width % step == 0:
            return step
    return width


def attend(peers, lens_in, queries_in, new_key_in, new_value_in, keys, values, *refs):
    count = (len(refs) - 8 - peers) // 2
    carried_in, outs = refs[:count], refs[count : count + peers]
    carried_out = refs[count + peers : 2 * count + peers]
    lens, queries, new_key, new_value, key_buf, value_buf, shares, sems = refs[-8:]
    slots, span, width = key_buf.shape
    kv_here = width // HEAD_DIM
    group = queries.shape[1] // width
    rows = group * slots
    small = [(lens_in, lens), (queries_in, queries), (new_key_in, new_key)]
    small.append((new_value_in, new_value))
    pairs = small + [(keys.at[s], key_buf.at[s]) for s in range(slots)]
    pairs += [(values.at[s], value_buf.at[s]) for s in range(slots)]
    for a, b in zip(carried_in, carried_out):
        if a.shape == b.shape:
            pairs.append((a, b))
        else:
            part = b.shape[2]
            pairs += [(a.at[:, pl.ds(p * part, part)], b.at[p]) for p in range(b.shape[0])]
    loads = [pltpu.make_async_copy(a, b, sems.at[i]) for i, (a, b) in enumerate(pairs)]
    for load in loads:
        load.start()
    for load in loads[: len(small)]:
        load.wait()
    loads = loads[len(small) :]
    scale = HEAD_DIM ** (-0.5)
    slot_id = lax.rem(lax.broadcasted_iota(jnp.int32, (rows, 1), 0), slots)
    live_len = jnp.zeros((rows, 1), jnp.int32)
    for s in range(slots):
        live_len = jnp.where(slot_id == s, lens[s], live_len)
    live = lax.broadcasted_iota(jnp.int32, (rows, span), 1) < live_len
    q_all = queries[...].astype(F32)
    own_k = new_key[...].astype(F32)
    own_v = new_value[...].astype(F32)
    heads_q, own_score = [], []
    for g in range(kv_here):
        cols = slice(g * HEAD_DIM, (g + 1) * HEAD_DIM)
        first = g * group
        q = jnp.concatenate(
            [
                q_all[:, (first + h) * HEAD_DIM : (first + h + 1) * HEAD_DIM]
                for h in range(group)
            ],
            axis=0,
        )
        k = jnp.concatenate([own_k[:, cols]] * group, axis=0)
        own_score.append(jnp.sum(q * k, axis=1, keepdims=True) * scale)
        heads_q.append(q.astype(BF16))
    scores = [jnp.zeros((rows, span), F32) for _ in range(kv_here)]
    for s in range(slots):
        loads[s].wait()
        for g in range(kv_here):
            here = lax.dot_general(
                heads_q[g],
                key_buf[s, :, g * HEAD_DIM : (g + 1) * HEAD_DIM],
                (((1,), (1,)), ((), ())),
                preferred_element_type=F32,
            )
            scores[g] = jnp.where(slot_id == s, here, scores[g])
    probs, totals = [], []
    for g in range(kv_here):
        masked = jnp.where(live, scores[g] * scale, -jnp.inf)
        top = jnp.maximum(jnp.max(masked, axis=1, keepdims=True), own_score[g])
        exp_cache = jnp.exp(masked - top)
        exp_own = jnp.exp(own_score[g] - top)
        total = jnp.sum(exp_cache, axis=1, keepdims=True) + exp_own
        probs.append((exp_cache / total).astype(BF16))
        own = jnp.concatenate(
            [own_v[:, g * HEAD_DIM : (g + 1) * HEAD_DIM]] * group, axis=0
        )
        totals.append((exp_own / total).astype(BF16).astype(F32) * own)
    for s in range(slots):
        loads[slots + s].wait()
        for g in range(kv_here):
            here = jnp.where(slot_id == s, probs[g], jnp.zeros_like(probs[g]))
            totals[g] += jnp.dot(
                here,
                value_buf[s, :, g * HEAD_DIM : (g + 1) * HEAD_DIM],
                preferred_element_type=F32,
            )
    heads_out = group // peers
    for f in range(peers):
        shares[f] = jnp.concatenate(
            [
                jnp.concatenate(
                    [totals[g][h * slots : (h + 1) * slots] for g in range(kv_here)], axis=0
                )
                for h in range(f * heads_out, (f + 1) * heads_out)
            ],
            axis=1,
        )
    mine = lax.axis_index("ffn")
    for f in range(peers):
        outs[f][...] = shares[mine ^ f].astype(BF16)
    for load in loads[2 * slots :]:
        load.wait()


def stack(count, *refs):
    out = refs[-1]
    for i, ref in enumerate(refs[:count]):
        out[i] = ref[...]


def add(count, *refs):
    total = refs[0][...].astype(F32)
    for ref in refs[1:count]:
        total += ref[...].astype(F32)
    refs[-1][...] = total.astype(BF16)


def project(slots, peers, slot_of, weight, *refs):
    refs, outs, parts = refs[: -1 - peers], refs[-1 - peers : -1], refs[-1]
    requests = slot_of.shape[1]
    _, rows, width = refs[0].shape
    kv_here = weight.shape[0]
    table = [ref[...].astype(F32).reshape(ref.shape[0] * rows, width) for ref in refs]
    table = jnp.concatenate(table, axis=0).astype(BF16)
    slot = slot_of[...]
    mine = lax.axis_index(("tok", "ffn"))
    where_from = ((slot // slots) ^ mine) * rows + lax.rem(slot, slots)
    row = lax.broadcasted_iota(jnp.int32, (table.shape[0], requests), 0)
    ordered = []
    for g in range(kv_here):
        pick = (row == where_from + g * slots).astype(F32).astype(BF16)
        ordered.append(
            lax.dot_general(
                pick, table, (((0,), (0,)), ((), ())), preferred_element_type=F32
            ).astype(BF16)
        )
    width = parts.shape[2]
    step = column_step(width)
    for p in range(peers):
        for c in range(0, width, step):
            at = p * width + c
            total = jnp.zeros((requests, step), F32)
            for g in range(kv_here):
                total += jnp.dot(
                    ordered[g], weight[g, :, at : at + step], preferred_element_type=F32
                )
            parts[p, :, c : c + step] = total
    core = lax.axis_index("rep")
    for p, out in enumerate(outs):
        out[...] = parts[core ^ p].astype(BF16)


def by_owner(value, ordered):
    blocks, rows, _ = ordered.shape
    mine = lax.axis_index("tok")
    for k in range(blocks):
        ordered[k] = value[k * rows : (k + 1) * rows]
    return jnp.concatenate([ordered[mine ^ k] for k in range(blocks)], axis=0)


def part_rows(peer, height):
    return pl.ds(pl.multiple_of((lax.axis_index("rep") ^ peer) * height, height), height)


def own_part(core, mid, gain, weight, left, sums, ordered):
    @pl.when(lax.axis_index("rep") == core)
    def _():
        scaled = mid[...].astype(F32) * gain[core]
        rhs = by_owner(scaled, ordered).astype(BF16)
        left[...] = rhs
        height = mid.shape[1]
        step = column_step(weight.shape[1])
        for c in range(0, weight.shape[1], step):
            sums[:, c : c + step] = jnp.dot(
                rhs,
                weight[core * height : (core + 1) * height, c : c + step],
                preferred_element_type=F32,
            )


def gate_first(core, residual, gain, weight, later, *refs):
    mid, left, sums, ordered = refs[-4:]
    total = residual[lax.axis_index("rep")].astype(F32)
    for ref in refs[:-4]:
        total += ref[...].astype(F32)
    mid[...] = total.astype(BF16)
    own_part(core, mid, gain, weight, left, sums, ordered)


def gate_next(core, mid, gain, weight, left_in, sums_in, left, sums, ordered):
    own_part(core, mid, gain, weight, left, sums, ordered)


def up_own(left, weight, sums):
    rhs = left[...]
    at = part_rows(0, left.shape[1])
    step = column_step(weight.shape[1])
    for c in range(0, weight.shape[1], step):
        sums[:, c : c + step] = jnp.dot(
            rhs, weight[at, c : c + step], preferred_element_type=F32
        )


def gate_rest(peers, *refs):
    mids = refs[:peers]
    gain, weight, sums, mid_out, left, stat_out, out, ordered, squares = refs[peers:]
    blocks, rows, height = ordered.shape
    core = lax.axis_index("rep")
    share = mid_out.shape[2]
    square = jnp.zeros((blocks * rows, 1), F32)
    lefts = []
    for p in range(peers):
        mid = mids[p][...].astype(F32)
        for j in range(mid_out.shape[1]):
            mid_out[core ^ p, j] = mid[j * share : (j + 1) * share].astype(BF16)
        square += jnp.sum(mid * mid, axis=1, keepdims=True)
        if p > 0:
            scaled = by_owner(mid * gain[core ^ p], ordered).astype(BF16)
            left[p - 1] = scaled
            lefts.append(scaled)
    square = by_owner(jnp.broadcast_to(square, (blocks * rows, 128)), squares)
    high = square.astype(BF16).astype(F32)
    medium = (square - high).astype(BF16).astype(F32)
    low = square - high - medium
    lane = lax.broadcasted_iota(jnp.int32, square.shape, 1)
    stat = jnp.where(lane == 0, high, jnp.where(lane == 1, medium, low))
    stat = jnp.where(lane < 3, stat, 0.0).astype(BF16)
    for k in range(blocks):
        stat_out[k] = stat[k * rows : (k + 1) * rows]
    width = weight.shape[1]
    step = column_step(width)
    for c in range(0, width, step):
        total = sums[:, c : c + step]
        for p in range(1, peers):
            total += jnp.dot(
                lefts[p - 1],
                weight[part_rows(p, height), c : c + step],
                preferred_element_type=F32,
            )
        for k in range(blocks):
            out[k, :, c : c + step] = total[k * rows : (k + 1) * rows].astype(BF16)


def up_rest(sums, rest, stat, gates, weight, *parts):
    rows = parts[0].shape[0]
    height, width = rest.shape[2], weight.shape[1]
    for k, part in enumerate(parts):
        part[:, :width] = gates[k]
        part[:, 2 * width :] = stat[k]
    lefts = [rest[p] for p in range(rest.shape[0])]
    step = column_step(width)
    for c in range(0, width, step):
        total = sums[:, c : c + step]
        for p, left in enumerate(lefts):
            total += jnp.dot(
                left, weight[part_rows(p + 1, height), c : c + step], preferred_element_type=F32
            )
        for k, part in enumerate(parts):
            part[:, width + c : width + c + step] = total[k * rows : (k + 1) * rows].astype(BF16)


def activate(features, *refs):
    out = refs[-1]
    width = out.shape[1]
    total = refs[0][...].astype(F32)
    for part in refs[1:-1]:
        total += part[...].astype(F32)
    square = jnp.sum(total[:, 2 * width :], axis=1, keepdims=True)
    inv_rms = lax.rsqrt(square / features + 1e-05)
    gate = total[:, :width] * inv_rms
    up = total[:, width : 2 * width] * inv_rms
    out[...] = (gate / (1.0 + jnp.exp(-gate)) * up).astype(BF16)


def down(blocks, pieces, *refs):
    parts = refs[:blocks]
    weights = refs[blocks : blocks + pieces]
    outs = refs[blocks + pieces : -1]
    ordered = refs[-1]
    mine, group = lax.axis_index("tok"), lax.axis_index(("ffn", "rep"))
    rows = parts[0].shape[0]
    share = outs[0].shape[0]
    for k in range(blocks):
        at = pl.multiple_of((mine ^ k) * rows, 8)
        ordered[pl.ds(at, rows)] = parts[k][...].astype(F32)
    left = jnp.concatenate(
        [
            ordered[pl.ds(pl.multiple_of((group ^ j) * share, 8), share)]
            for j in range(len(outs))
        ],
        axis=0,
    ).astype(BF16)
    base = 0
    for weight in weights:
        width = weight.shape[1]
        step = column_step(width)
        for c in range(0, width, step):
            total = jnp.dot(left, weight[:, c : c + step], preferred_element_type=F32)
            for j, out in enumerate(outs):
                at = base + c
                out[:, at : at + step] = total[j * share : (j + 1) * share].astype(BF16)
        base += width


def finish(mid, *refs):
    mine = lax.axis_index(("ffn", "rep"))
    out = refs[-1]
    total = jnp.concatenate([mid[p, mine] for p in range(mid.shape[0])], axis=1).astype(F32)
    for part in refs[:-1]:
        total += part[...].astype(F32)
    out[...] = total.astype(BF16)


def like(*shape):
    return jax.ShapeDtypeStruct(shape, BF16)


def limit(mib):
    return pltpu.CompilerParams(vmem_limit_bytes=mib * MIB)


def shards(
    queries,
    new_key,
    new_value,
    key_cache,
    value_cache,
    lengths,
    slot_of,
    residual_in,
    out_weight,
    norm_gain,
    gate_weight,
    up_weight,
    down_weight,
):
    tok, ffn, rep = (lax.axis_size(a) for a in ("tok", "ffn", "rep"))
    sums = ffn * rep
    slots, span, kv_width = key_cache.shape
    kv_here = kv_width // HEAD_DIM
    requests, features = residual_in.shape
    hidden_here = gate_weight.shape[1]
    feat_width = out_weight.shape[1]
    in_hbm = functools.partial(pltpu.with_memory_space_constraint, memory_space=pltpu.HBM)

    height = features // rep
    slot_of = slot_of.reshape(1, requests)
    carried = [
        slot_of,
        residual_in,
        norm_gain.reshape(1, features),
    ]
    table_rows = slots * kv_here
    *attended, slot_of, residual_in, norm_gain = pl.pallas_call(
        functools.partial(attend, ffn),
        out_shape=[like(table_rows, feat_width)] * ffn
        + [
            pltpu.VMEM(slot_of.shape, slot_of.dtype),
            pltpu.VMEM((rep, requests, height), BF16),
            pltpu.VMEM((rep, 1, height), F32),
        ],
        in_specs=[HBM] * (6 + len(carried)),
        out_specs=[VMEM] * (ffn + len(carried)),
        scratch_shapes=[
            pltpu.SMEM(lengths.shape, jnp.int32),
            pltpu.VMEM(queries.shape, BF16),
            pltpu.VMEM(new_key.shape, BF16),
            pltpu.VMEM(new_value.shape, BF16),
            pltpu.VMEM(key_cache.shape, BF16),
            pltpu.VMEM(value_cache.shape, BF16),
            pltpu.VMEM((ffn, table_rows, feat_width), F32),
            pltpu.SemaphoreType.DMA((5 + 2 * slots + 2 * rep,)),
        ],
        compiler_params=limit(3),
        cost_estimate=pl.CostEstimate(flops=20000000000, transcendentals=0, bytes_accessed=0),
        name="attend",
    )(
        *(
            in_hbm(a)
            for a in [lengths, queries, new_key, new_value, key_cache, value_cache] + carried
        )
    )
    owners = tok * ffn
    near = min(2, tok)
    out_weight = pltpu.with_memory_space_constraint(out_weight, pltpu.VMEM)
    in_vmem = functools.partial(pltpu.with_memory_space_constraint, memory_space=pltpu.VMEM)
    close = [None] * (near * ffn)
    for k in reversed(range(near * ffn)):
        close[k] = lax.ppermute(
            attended[k % ffn], ("tok", "ffn", "rep"), swap(owners * rep, k * rep + rep - 1)
        )
    gate_weight = in_vmem(gate_weight)
    close = pl.pallas_call(
        functools.partial(stack, near * ffn),
        out_shape=like(near * ffn, table_rows, feat_width),
        in_specs=[VMEM] * (near * ffn + 1),
        out_specs=VMEM,
        compiler_params=limit(3),
        name="stack",
    )(*close, gate_weight)
    gathered = [
        lax.ppermute(close, ("tok", "rep"), swap(tok * rep, k * rep + rep - 1))
        for k in range(0, tok, near)
    ]

    partials = pl.pallas_call(
        functools.partial(project, slots, rep),
        out_shape=[like(requests, height)] * rep,
        in_specs=[VMEM] * (2 + len(gathered)),
        out_specs=[VMEM] * rep,
        scratch_shapes=[pltpu.VMEM((rep, requests, height), F32)],
        compiler_params=limit(3),
        cost_estimate=pl.CostEstimate(flops=10000000000, transcendentals=0, bytes_accessed=0),
        name="project",
    )(slot_of, out_weight, *gathered)
    summed = [partials[0]] + [
        lax.ppermute(partials[k], "rep", swap(rep, k)) for k in range(1, rep)
    ]
    here = pl.pallas_call(
        functools.partial(add, len(summed)),
        out_shape=like(requests, height),
        in_specs=[VMEM] * len(summed),
        out_specs=VMEM,
        compiler_params=limit(3),
        name="add",
    )(*summed)
    arrived = [lax.ppermute(here, "ffn", swap(ffn, k)) for k in range(1, ffn)]
    rows = requests // tok
    share = requests // sums
    up_weight = in_vmem(up_weight)
    own_shapes = [like(requests, height), jax.ShapeDtypeStruct((requests, hidden_here), F32)]
    mid_own, own, own_sums = pl.pallas_call(
        functools.partial(gate_first, rep - 1),
        out_shape=[like(requests, height)] + own_shapes,
        in_specs=[VMEM] * (4 + ffn),
        out_specs=[VMEM] * 3,
        scratch_shapes=[pltpu.VMEM((tok, rows, height), F32)],
        compiler_params=limit(3),
        name="gate_first",
    )(residual_in, norm_gain, gate_weight, up_weight, here, *arrived)
    mids = [mid_own] + [lax.ppermute(mid_own, "rep", swap(rep, k)) for k in range(1, rep)]
    for core in reversed(range(rep - 1)):
        own, own_sums = pl.pallas_call(
            functools.partial(gate_next, core),
            out_shape=own_shapes,
            in_specs=[VMEM] * 5,
            out_specs=[VMEM] * 2,
            input_output_aliases={3: 0, 4: 1},
            scratch_shapes=[pltpu.VMEM((tok, rows, height), F32)],
            compiler_params=limit(3),
            name="gate_next",
        )(mid_own, norm_gain, gate_weight, own, own_sums)
    up_sums = pl.pallas_call(
        up_own,
        out_shape=own_shapes[1],
        in_specs=[VMEM] * 2,
        out_specs=VMEM,
        compiler_params=limit(3),
        name="up_own",
    )(own, up_weight)
    mid, rest, stat, gates = pl.pallas_call(
        functools.partial(gate_rest, rep),
        out_shape=[
            like(rep, sums, share, height),
            like(rep - 1, requests, height),
            like(tok, rows, 128),
            like(tok, rows, hidden_here),
        ],
        in_specs=[VMEM] * (3 + rep),
        out_specs=[VMEM] * 4,
        scratch_shapes=[
            pltpu.VMEM((tok, rows, height), F32),
            pltpu.VMEM((tok, rows, 128), F32),
        ],
        compiler_params=limit(3),
        name="gate_rest",
    )(*mids, norm_gain, gate_weight, own_sums)
    parts = pl.pallas_call(
        up_rest,
        out_shape=[like(rows, 2 * hidden_here + 128)] * tok,
        in_specs=[VMEM] * 5,
        out_specs=[VMEM] * tok,
        compiler_params=limit(3),
        name="up_rest",
    )(up_sums, rest, stat, gates, up_weight)
    order = sorted(range(1, tok), reverse=True)
    got = [parts[0]] + [lax.ppermute(parts[k], "tok", swap(tok, k)) for k in order]

    hidden = pl.pallas_call(
        functools.partial(activate, features * tok),
        out_shape=like(rows, hidden_here),
        in_specs=[VMEM] * tok,
        out_specs=VMEM,
        compiler_params=limit(3),
        name="activate",
    )(*got)
    pieces = {k: lax.ppermute(hidden, "tok", swap(tok, k)) for k in sorted(range(1, tok), reverse=True)}

    downs = pl.pallas_call(
        functools.partial(down, tok, 1),
        out_shape=[like(share, features)] * sums,
        in_specs=[VMEM] * (1 + tok),
        out_specs=[VMEM] * sums,
        scratch_shapes=[pltpu.VMEM((requests, hidden_here), F32)],
        compiler_params=limit(3),
        name="down",
    )(hidden, *[pieces[k] for k in range(1, tok)], in_vmem(down_weight))
    order = sorted(range(1, sums), reverse=True)
    got = [downs[0]] + [lax.ppermute(downs[j], ("ffn", "rep"), swap(sums, j)) for j in order]

    return pl.pallas_call(
        finish,
        out_shape=like(share, features),
        in_specs=[VMEM] * (1 + sums),
        out_specs=VMEM,
        compiler_params=limit(3),
        name="finish",
    )(mid, *got)


def solution(mesh):
    placed = (
        P(("groups", "tok", "ffn"), "rep"),
        P(("groups", "tok", "ffn"), "rep"),
        P(("groups", "tok", "ffn"), "rep"),
        P(("groups", "tok", "ffn"), None, "rep"),
        P(("groups", "tok", "ffn"), None, "rep"),
        P(("groups", "tok", "ffn")),
        P("groups"),
        P("groups", "tok"),
        P("rep", "ffn", "tok"),
        P("tok"),
        P("tok", ("ffn", "rep")),
        P("tok", ("ffn", "rep")),
        P(("ffn", "rep"), "tok"),
    )
    return jax.shard_map(
        shards,
        mesh=mesh,
        in_specs=placed,
        out_specs=P(("groups", "ffn", "rep"), "tok"),
        check_vma=False,
    )
```

```python
import functools

import jax
import jax.numpy as jnp
from jax import lax
from jax.experimental import pallas as pl
from jax.experimental.pallas import tpu as pltpu
from jax.sharding import PartitionSpec as P

HEAD_DIM = 128
F32 = jnp.float32
BF16 = jnp.bfloat16
MIB = 2**20
VMEM = pl.BlockSpec(memory_space=pltpu.VMEM)
SMEM = pl.BlockSpec(memory_space=pltpu.SMEM)
ANY = pl.BlockSpec(memory_space=pl.ANY)
HBM = ANY


def swap(extent, step):
    return [(a, a ^ step) for a in range(extent)]


def column_step(width):
    for step in (896, 512, 256, 128):
        if width % step == 0:
            return step
    return width


def attend(peers, lens_in, queries_in, new_key_in, new_value_in, keys, values, *refs):
    count = (len(refs) - 8 - peers) // 2
    carried_in, outs = refs[:count], refs[count : count + peers]
    carried_out = refs[count + peers : 2 * count + peers]
    lens, queries, new_key, new_value, key_buf, value_buf, shares, sems = refs[-8:]
    slots, span, width = key_buf.shape
    kv_here = width // HEAD_DIM
    group = queries.shape[1] // width
    rows = group * slots
    small = [(lens_in, lens), (queries_in, queries), (new_key_in, new_key)]
    small.append((new_value_in, new_value))
    pairs = small + [(keys.at[s], key_buf.at[s]) for s in range(slots)]
    pairs += [(values.at[s], value_buf.at[s]) for s in range(slots)]
    for a, b in zip(carried_in, carried_out):
        if a.shape == b.shape:
            pairs.append((a, b))
        else:
            part = b.shape[2]
            pairs += [(a.at[:, pl.ds(p * part, part)], b.at[p]) for p in range(b.shape[0])]
    loads = [pltpu.make_async_copy(a, b, sems.at[i]) for i, (a, b) in enumerate(pairs)]
    for load in loads:
        load.start()
    for load in loads[: len(small)]:
        load.wait()
    loads = loads[len(small) :]
    scale = HEAD_DIM ** (-0.5)
    slot_id = lax.rem(lax.broadcasted_iota(jnp.int32, (rows, 1), 0), slots)
    live_len = jnp.zeros((rows, 1), jnp.int32)
    for s in range(slots):
        live_len = jnp.where(slot_id == s, lens[s], live_len)
    live = lax.broadcasted_iota(jnp.int32, (rows, span), 1) < live_len
    q_all = queries[...].astype(F32)
    own_k = new_key[...].astype(F32)
    own_v = new_value[...].astype(F32)
    heads_q, own_score = [], []
    for g in range(kv_here):
        cols = slice(g * HEAD_DIM, (g + 1) * HEAD_DIM)
        first = g * group
        q = jnp.concatenate(
            [
                q_all[:, (first + h) * HEAD_DIM : (first + h + 1) * HEAD_DIM]
                for h in range(group)
            ],
            axis=0,
        )
        k = jnp.concatenate([own_k[:, cols]] * group, axis=0)
        own_score.append(jnp.sum(q * k, axis=1, keepdims=True) * scale)
        heads_q.append(q.astype(BF16))
    scores = [jnp.zeros((rows, span), F32) for _ in range(kv_here)]
    for s in range(slots):
        loads[s].wait()
        for g in range(kv_here):
            here = lax.dot_general(
                heads_q[g],
                key_buf[s, :, g * HEAD_DIM : (g + 1) * HEAD_DIM],
                (((1,), (1,)), ((), ())),
                preferred_element_type=F32,
            )
            scores[g] = jnp.where(slot_id == s, here, scores[g])
    probs, totals = [], []
    for g in range(kv_here):
        masked = jnp.where(live, scores[g] * scale, -jnp.inf)
        top = jnp.maximum(jnp.max(masked, axis=1, keepdims=True), own_score[g])
        exp_cache = jnp.exp(masked - top)
        exp_own = jnp.exp(own_score[g] - top)
        total = jnp.sum(exp_cache, axis=1, keepdims=True) + exp_own
        probs.append((exp_cache / total).astype(BF16))
        own = jnp.concatenate(
            [own_v[:, g * HEAD_DIM : (g + 1) * HEAD_DIM]] * group, axis=0
        )
        totals.append((exp_own / total).astype(BF16).astype(F32) * own)
    for s in range(slots):
        loads[slots + s].wait()
        for g in range(kv_here):
            here = jnp.where(slot_id == s, probs[g], jnp.zeros_like(probs[g]))
            totals[g] += jnp.dot(
                here,
                value_buf[s, :, g * HEAD_DIM : (g + 1) * HEAD_DIM],
                preferred_element_type=F32,
            )
    heads_out = group // peers
    for f in range(peers):
        shares[f] = jnp.concatenate(
            [
                jnp.concatenate(
                    [totals[g][h * slots : (h + 1) * slots] for g in range(kv_here)], axis=0
                )
                for h in range(f * heads_out, (f + 1) * heads_out)
            ],
            axis=1,
        )
    mine = lax.axis_index("ffn")
    for f in range(peers):
        outs[f][...] = shares[mine ^ f].astype(BF16)
    for load in loads[2 * slots :]:
        load.wait()


def stack(count, *refs):
    out = refs[-1]
    for i, ref in enumerate(refs[:count]):
        out[i] = ref[...]


def add(count, *refs):
    total = refs[0][...].astype(F32)
    for ref in refs[1:count]:
        total += ref[...].astype(F32)
    refs[-1][...] = total.astype(BF16)


def project(slots, peers, slot_of, weight, *refs):
    refs, outs, table_out = refs[:-peers], refs[-peers:-1], refs[-1]
    requests = slot_of.shape[1]
    _, rows, width = refs[0].shape
    kv_here = weight.shape[0]
    table = [ref[...].astype(F32).reshape(ref.shape[0] * rows, width) for ref in refs]
    table = jnp.concatenate(table, axis=0).astype(BF16)
    slot = slot_of[...]
    mine = lax.axis_index(("tok", "ffn"))
    where_from = ((slot // slots) ^ mine) * rows + lax.rem(slot, slots)
    row = lax.broadcasted_iota(jnp.int32, (table.shape[0], requests), 0)
    for g in range(kv_here):
        pick = (row == where_from + g * slots).astype(F32).astype(BF16)
        table_out[g] = lax.dot_general(
            pick, table, (((0,), (0,)), ((), ())), preferred_element_type=F32
        ).astype(BF16)
    for p, out in enumerate(outs):
        project_part(p + 1, table_out, weight, out)


def project_part(peer, ordered, weight, out):
    width = out.shape[1]
    step = column_step(width)
    first = (lax.axis_index("rep") ^ peer) * width
    for c in range(0, width, step):
        at = pl.ds(pl.multiple_of(first + c, 128), step)
        total = jnp.zeros((out.shape[0], step), F32)
        for g in range(weight.shape[0]):
            total += jnp.dot(ordered[g], weight[g, :, at], preferred_element_type=F32)
        out[:, c : c + step] = total.astype(BF16)


def by_owner(value, ordered):
    blocks, rows, _ = ordered.shape
    mine = lax.axis_index("tok")
    for k in range(blocks):
        ordered[k] = value[k * rows : (k + 1) * rows]
    return jnp.concatenate([ordered[mine ^ k] for k in range(blocks)], axis=0)


def part_rows(peer, height):
    return pl.ds(pl.multiple_of((lax.axis_index("rep") ^ peer) * height, height), height)


def own_part(core, mid, gain, weight, left, sums, ordered):
    @pl.when(lax.axis_index("rep") == core)
    def _():
        scaled = mid[...].astype(F32) * gain[core]
        rhs = by_owner(scaled, ordered).astype(BF16)
        left[...] = rhs
        height = mid.shape[1]
        step = column_step(weight.shape[1])
        for c in range(0, weight.shape[1], step):
            sums[:, c : c + step] = jnp.dot(
                rhs,
                weight[core * height : (core + 1) * height, c : c + step],
                preferred_element_type=F32,
            )


def gate_first(core, residual, gain, weight, later, *refs):
    mid, left, sums, ordered = refs[-4:]
    total = residual[lax.axis_index("rep")].astype(F32)
    for ref in refs[:-4]:
        total += ref[...].astype(F32)
    mid[...] = total.astype(BF16)
    own_part(core, mid, gain, weight, left, sums, ordered)


def gate_next(core, mid, gain, weight, left_in, sums_in, left, sums, ordered):
    own_part(core, mid, gain, weight, left, sums, ordered)


def up_own(left, weight, sums):
    rhs = left[...]
    at = part_rows(0, left.shape[1])
    step = column_step(weight.shape[1])
    for c in range(0, weight.shape[1], step):
        sums[:, c : c + step] = jnp.dot(
            rhs, weight[at, c : c + step], preferred_element_type=F32
        )


def gate_rest(peers, *refs):
    mids = refs[:peers]
    gain, weight, sums, mid_out, left, stat_out, out, ordered, squares = refs[peers:]
    blocks, rows, height = ordered.shape
    core = lax.axis_index("rep")
    share = mid_out.shape[2]
    square = jnp.zeros((blocks * rows, 1), F32)
    lefts = []
    for p in range(peers):
        mid = mids[p][...].astype(F32)
        for j in range(mid_out.shape[1]):
            mid_out[core ^ p, j] = mid[j * share : (j + 1) * share].astype(BF16)
        square += jnp.sum(mid * mid, axis=1, keepdims=True)
        if p > 0:
            scaled = by_owner(mid * gain[core ^ p], ordered).astype(BF16)
            left[p - 1] = scaled
            lefts.append(scaled)
    square = by_owner(jnp.broadcast_to(square, (blocks * rows, 128)), squares)
    high = square.astype(BF16).astype(F32)
    medium = (square - high).astype(BF16).astype(F32)
    low = square - high - medium
    lane = lax.broadcasted_iota(jnp.int32, square.shape, 1)
    stat = jnp.where(lane == 0, high, jnp.where(lane == 1, medium, low))
    stat = jnp.where(lane < 3, stat, 0.0).astype(BF16)
    for k in range(blocks):
        stat_out[k] = stat[k * rows : (k + 1) * rows]
    width = weight.shape[1]
    step = column_step(width)
    for c in range(0, width, step):
        total = sums[:, c : c + step]
        for p in range(1, peers):
            total += jnp.dot(
                lefts[p - 1],
                weight[part_rows(p, height), c : c + step],
                preferred_element_type=F32,
            )
        for k in range(blocks):
            out[k, :, c : c + step] = total[k * rows : (k + 1) * rows].astype(BF16)


def up_rest(sums, rest, stat, gates, weight, *parts):
    rows = parts[0].shape[0]
    height, width = rest.shape[2], weight.shape[1]
    for k, part in enumerate(parts):
        part[:, :width] = gates[k]
        part[:, 2 * width :] = stat[k]
    lefts = [rest[p] for p in range(rest.shape[0])]
    step = column_step(width)
    for c in range(0, width, step):
        total = sums[:, c : c + step]
        for p, left in enumerate(lefts):
            total += jnp.dot(
                left, weight[part_rows(p + 1, height), c : c + step], preferred_element_type=F32
            )
        for k, part in enumerate(parts):
            part[:, width + c : width + c + step] = total[k * rows : (k + 1) * rows].astype(BF16)


def activate(features, *refs):
    out = refs[-1]
    width = out.shape[1]
    total = refs[0][...].astype(F32)
    for part in refs[1:-1]:
        total += part[...].astype(F32)
    square = jnp.sum(total[:, 2 * width :], axis=1, keepdims=True)
    inv_rms = lax.rsqrt(square / features + 1e-05)
    gate = total[:, :width] * inv_rms
    up = total[:, width : 2 * width] * inv_rms
    out[...] = (gate / (1.0 + jnp.exp(-gate)) * up).astype(BF16)


def down(blocks, pieces, *refs):
    parts = refs[:blocks]
    weights = refs[blocks : blocks + pieces]
    outs = refs[blocks + pieces : -1]
    ordered = refs[-1]
    mine, group = lax.axis_index("tok"), lax.axis_index(("ffn", "rep"))
    rows = parts[0].shape[0]
    share = outs[0].shape[0]
    for k in range(blocks):
        at = pl.multiple_of((mine ^ k) * rows, 8)
        ordered[pl.ds(at, rows)] = parts[k][...].astype(F32)
    left = jnp.concatenate(
        [
            ordered[pl.ds(pl.multiple_of((group ^ j) * share, 8), share)]
            for j in range(len(outs))
        ],
        axis=0,
    ).astype(BF16)
    base = 0
    for weight in weights:
        width = weight.shape[1]
        step = column_step(width)
        for c in range(0, width, step):
            total = jnp.dot(left, weight[:, c : c + step], preferred_element_type=F32)
            for j, out in enumerate(outs):
                at = base + c
                out[:, at : at + step] = total[j * share : (j + 1) * share].astype(BF16)
        base += width


def finish(mid, *refs):
    mine = lax.axis_index(("ffn", "rep"))
    out = refs[-1]
    total = jnp.concatenate([mid[p, mine] for p in range(mid.shape[0])], axis=1).astype(F32)
    for part in refs[:-1]:
        total += part[...].astype(F32)
    out[...] = total.astype(BF16)


def like(*shape):
    return jax.ShapeDtypeStruct(shape, BF16)


def limit(mib):
    return pltpu.CompilerParams(vmem_limit_bytes=mib * MIB)


def shards(
    queries,
    new_key,
    new_value,
    key_cache,
    value_cache,
    lengths,
    slot_of,
    residual_in,
    out_weight,
    norm_gain,
    gate_weight,
    up_weight,
    down_weight,
):
    tok, ffn, rep = (lax.axis_size(a) for a in ("tok", "ffn", "rep"))
    sums = ffn * rep
    slots, span, kv_width = key_cache.shape
    kv_here = kv_width // HEAD_DIM
    requests, features = residual_in.shape
    hidden_here = gate_weight.shape[1]
    feat_width = out_weight.shape[1]
    in_hbm = functools.partial(pltpu.with_memory_space_constraint, memory_space=pltpu.HBM)

    height = features // rep
    slot_of = slot_of.reshape(1, requests)
    carried = [
        slot_of,
        residual_in,
        norm_gain.reshape(1, features),
    ]
    table_rows = slots * kv_here
    *attended, slot_of, residual_in, norm_gain = pl.pallas_call(
        functools.partial(attend, ffn),
        out_shape=[like(table_rows, feat_width)] * ffn
        + [
            pltpu.VMEM(slot_of.shape, slot_of.dtype),
            pltpu.VMEM((rep, requests, height), BF16),
            pltpu.VMEM((rep, 1, height), F32),
        ],
        in_specs=[HBM] * (6 + len(carried)),
        out_specs=[VMEM] * (ffn + len(carried)),
        scratch_shapes=[
            pltpu.SMEM(lengths.shape, jnp.int32),
            pltpu.VMEM(queries.shape, BF16),
            pltpu.VMEM(new_key.shape, BF16),
            pltpu.VMEM(new_value.shape, BF16),
            pltpu.VMEM(key_cache.shape, BF16),
            pltpu.VMEM(value_cache.shape, BF16),
            pltpu.VMEM((ffn, table_rows, feat_width), F32),
            pltpu.SemaphoreType.DMA((5 + 2 * slots + 2 * rep,)),
        ],
        compiler_params=limit(3),
        cost_estimate=pl.CostEstimate(flops=20000000000, transcendentals=0, bytes_accessed=0),
        name="attend",
    )(
        *(
            in_hbm(a)
            for a in [lengths, queries, new_key, new_value, key_cache, value_cache] + carried
        )
    )
    owners = tok * ffn
    near = min(2, tok)
    out_weight = pltpu.with_memory_space_constraint(out_weight, pltpu.VMEM)
    in_vmem = functools.partial(pltpu.with_memory_space_constraint, memory_space=pltpu.VMEM)
    close = [None] * (near * ffn)
    for k in reversed(range(near * ffn)):
        close[k] = lax.ppermute(
            attended[k % ffn], ("tok", "ffn", "rep"), swap(owners * rep, k * rep + rep - 1)
        )
    gate_weight = in_vmem(gate_weight)
    close = pl.pallas_call(
        functools.partial(stack, near * ffn),
        out_shape=like(near * ffn, table_rows, feat_width),
        in_specs=[VMEM] * (near * ffn + 1),
        out_specs=VMEM,
        compiler_params=limit(3),
        name="stack",
    )(*close, gate_weight)
    gathered = [
        lax.ppermute(close, ("tok", "rep"), swap(tok * rep, k * rep + rep - 1))
        for k in range(0, tok, near)
    ]

    *given, ordered = pl.pallas_call(
        functools.partial(project, slots, rep),
        out_shape=[like(requests, height)] * (rep - 1) + [like(kv_here, requests, feat_width)],
        in_specs=[VMEM] * (2 + len(gathered)),
        out_specs=[VMEM] * rep,
        compiler_params=limit(3),
        cost_estimate=pl.CostEstimate(flops=10000000000, transcendentals=0, bytes_accessed=0),
        name="project",
    )(slot_of, out_weight, *gathered)
    summed = [lax.ppermute(part, "rep", swap(rep, k + 1)) for k, part in enumerate(given)]
    kept = pl.pallas_call(
        functools.partial(project_part, 0),
        out_shape=like(requests, height),
        in_specs=[VMEM] * 2,
        out_specs=VMEM,
        compiler_params=limit(3),
        name="project_own",
    )(ordered, out_weight)
    summed = [kept] + summed
    here = pl.pallas_call(
        functools.partial(add, len(summed)),
        out_shape=like(requests, height),
        in_specs=[VMEM] * len(summed),
        out_specs=VMEM,
        compiler_params=limit(3),
        name="add",
    )(*summed)
    arrived = [lax.ppermute(here, "ffn", swap(ffn, k)) for k in range(1, ffn)]
    rows = requests // tok
    share = requests // sums
    up_weight = in_vmem(up_weight)
    own_shapes = [like(requests, height), jax.ShapeDtypeStruct((requests, hidden_here), F32)]
    mid_own, own, own_sums = pl.pallas_call(
        functools.partial(gate_first, rep - 1),
        out_shape=[like(requests, height)] + own_shapes,
        in_specs=[VMEM] * (4 + ffn),
        out_specs=[VMEM] * 3,
        scratch_shapes=[pltpu.VMEM((tok, rows, height), F32)],
        compiler_params=limit(3),
        name="gate_first",
    )(residual_in, norm_gain, gate_weight, up_weight, here, *arrived)
    mids = [mid_own] + [lax.ppermute(mid_own, "rep", swap(rep, k)) for k in range(1, rep)]
    for core in reversed(range(rep - 1)):
        own, own_sums = pl.pallas_call(
            functools.partial(gate_next, core),
            out_shape=own_shapes,
            in_specs=[VMEM] * 5,
            out_specs=[VMEM] * 2,
            input_output_aliases={3: 0, 4: 1},
            scratch_shapes=[pltpu.VMEM((tok, rows, height), F32)],
            compiler_params=limit(3),
            name="gate_next",
        )(mid_own, norm_gain, gate_weight, own, own_sums)
    up_sums = pl.pallas_call(
        up_own,
        out_shape=own_shapes[1],
        in_specs=[VMEM] * 2,
        out_specs=VMEM,
        compiler_params=limit(3),
        name="up_own",
    )(own, up_weight)
    mid, rest, stat, gates = pl.pallas_call(
        functools.partial(gate_rest, rep),
        out_shape=[
            like(rep, sums, share, height),
            like(rep - 1, requests, height),
            like(tok, rows, 128),
            like(tok, rows, hidden_here),
        ],
        in_specs=[VMEM] * (3 + rep),
        out_specs=[VMEM] * 4,
        scratch_shapes=[
            pltpu.VMEM((tok, rows, height), F32),
            pltpu.VMEM((tok, rows, 128), F32),
        ],
        compiler_params=limit(3),
        name="gate_rest",
    )(*mids, norm_gain, gate_weight, own_sums)
    parts = pl.pallas_call(
        up_rest,
        out_shape=[like(rows, 2 * hidden_here + 128)] * tok,
        in_specs=[VMEM] * 5,
        out_specs=[VMEM] * tok,
        compiler_params=limit(3),
        name="up_rest",
    )(up_sums, rest, stat, gates, up_weight)
    order = sorted(range(1, tok), reverse=True)
    got = [parts[0]] + [lax.ppermute(parts[k], "tok", swap(tok, k)) for k in order]

    hidden = pl.pallas_call(
        functools.partial(activate, features * tok),
        out_shape=like(rows, hidden_here),
        in_specs=[VMEM] * tok,
        out_specs=VMEM,
        compiler_params=limit(3),
        name="activate",
    )(*got)
    pieces = {k: lax.ppermute(hidden, "tok", swap(tok, k)) for k in sorted(range(1, tok), reverse=True)}

    downs = pl.pallas_call(
        functools.partial(down, tok, 1),
        out_shape=[like(share, features)] * sums,
        in_specs=[VMEM] * (1 + tok),
        out_specs=[VMEM] * sums,
        scratch_shapes=[pltpu.VMEM((requests, hidden_here), F32)],
        compiler_params=limit(3),
        name="down",
    )(hidden, *[pieces[k] for k in range(1, tok)], in_vmem(down_weight))
    order = sorted(range(1, sums), reverse=True)
    got = [downs[0]] + [lax.ppermute(downs[j], ("ffn", "rep"), swap(sums, j)) for j in order]

    return pl.pallas_call(
        finish,
        out_shape=like(share, features),
        in_specs=[VMEM] * (1 + sums),
        out_specs=VMEM,
        compiler_params=limit(3),
        name="finish",
    )(mid, *got)


def solution(mesh):
    placed = (
        P(("groups", "tok", "ffn"), "rep"),
        P(("groups", "tok", "ffn"), "rep"),
        P(("groups", "tok", "ffn"), "rep"),
        P(("groups", "tok", "ffn"), None, "rep"),
        P(("groups", "tok", "ffn"), None, "rep"),
        P(("groups", "tok", "ffn")),
        P("groups"),
        P("groups", "tok"),
        P("rep", "ffn", "tok"),
        P("tok"),
        P("tok", ("ffn", "rep")),
        P("tok", ("ffn", "rep")),
        P(("ffn", "rep"), "tok"),
    )
    return jax.shard_map(
        shards,
        mesh=mesh,
        in_specs=placed,
        out_specs=P(("groups", "ffn", "rep"), "tok"),
        check_vma=False,
    )
```

```python
import functools

import jax
import jax.numpy as jnp
from jax import lax
from jax.experimental import pallas as pl
from jax.experimental.pallas import tpu as pltpu
from jax.sharding import PartitionSpec as P

HEAD_DIM = 128
F32 = jnp.float32
BF16 = jnp.bfloat16
MIB = 2**20
VMEM = pl.BlockSpec(memory_space=pltpu.VMEM)
SMEM = pl.BlockSpec(memory_space=pltpu.SMEM)
ANY = pl.BlockSpec(memory_space=pl.ANY)
HBM = ANY


def swap(extent, step):
    return [(a, a ^ step) for a in range(extent)]


def column_step(width):
    for step in (896, 512, 256, 128):
        if width % step == 0:
            return step
    return width


def attend(peers, lens_in, queries_in, new_key_in, new_value_in, keys, values, *refs):
    count = (len(refs) - 8 - peers) // 2
    carried_in, outs = refs[:count], refs[count : count + peers]
    carried_out = refs[count + peers : 2 * count + peers]
    lens, queries, new_key, new_value, key_buf, value_buf, shares, sems = refs[-8:]
    slots, span, width = key_buf.shape
    kv_here = width // HEAD_DIM
    group = queries.shape[1] // width
    rows = kv_here * group * slots
    small = [(lens_in, lens), (queries_in, queries), (new_key_in, new_key)]
    small.append((new_value_in, new_value))
    pairs = small + [(keys.at[s], key_buf.at[s]) for s in range(slots)]
    pairs += [(values.at[s], value_buf.at[s]) for s in range(slots)]
    for a, b in zip(carried_in, carried_out):
        if a.shape == b.shape:
            pairs.append((a, b))
        else:
            part = b.shape[2]
            pairs += [(a.at[:, pl.ds(p * part, part)], b.at[p]) for p in range(b.shape[0])]
    loads = [pltpu.make_async_copy(a, b, sems.at[i]) for i, (a, b) in enumerate(pairs)]
    for load in loads:
        load.start()
    for load in loads[: len(small)]:
        load.wait()
    loads = loads[len(small) :]
    scale = HEAD_DIM ** (-0.5)
    slot_id = lax.rem(lax.broadcasted_iota(jnp.int32, (rows, 1), 0), slots)
    live_len = jnp.zeros((rows, 1), jnp.int32)
    for s in range(slots):
        live_len = jnp.where(slot_id == s, lens[s], live_len)
    live = lax.broadcasted_iota(jnp.int32, (rows, span), 1) < live_len
    kv_id = lax.broadcasted_iota(jnp.int32, (rows, width), 0) // (group * slots)
    mine = kv_id == lax.broadcasted_iota(jnp.int32, (rows, width), 1) // HEAD_DIM
    q_all = queries[...].astype(F32)
    heads = kv_here * group
    heads_q = jnp.concatenate(
        [q_all[:, h * HEAD_DIM : (h + 1) * HEAD_DIM] for h in range(heads)], axis=0
    )
    heads_q = jnp.where(mine, jnp.concatenate([heads_q] * kv_here, axis=1), 0.0)
    own_k = jnp.concatenate([new_key[...].astype(F32)] * heads, axis=0)
    own_v = jnp.concatenate([new_value[...].astype(F32)] * heads, axis=0)
    own_score = jnp.sum(heads_q * own_k, axis=1, keepdims=True) * scale
    heads_q = heads_q.astype(BF16)
    scores = jnp.zeros((rows, span), F32)
    for s in range(slots):
        loads[s].wait()
        here = lax.dot_general(
            heads_q, key_buf[s], (((1,), (1,)), ((), ())), preferred_element_type=F32
        )
        scores = jnp.where(slot_id == s, here, scores)
    masked = jnp.where(live, scores * scale, -jnp.inf)
    top = jnp.maximum(jnp.max(masked, axis=1, keepdims=True), own_score)
    exp_cache = jnp.exp(masked - top)
    exp_own = jnp.exp(own_score - top)
    total = jnp.sum(exp_cache, axis=1, keepdims=True) + exp_own
    probs = (exp_cache / total).astype(BF16)
    sums = (exp_own / total).astype(BF16).astype(F32) * own_v
    for s in range(slots):
        loads[slots + s].wait()
        here = jnp.where(slot_id == s, probs, jnp.zeros_like(probs))
        sums += jnp.dot(here, value_buf[s], preferred_element_type=F32)
    heads_out = group // peers
    for f in range(peers):
        shares[f] = jnp.concatenate(
            [
                jnp.concatenate(
                    [
                        sums[
                            (g * group + h) * slots : (g * group + h + 1) * slots,
                            g * HEAD_DIM : (g + 1) * HEAD_DIM,
                        ]
                        for g in range(kv_here)
                    ],
                    axis=0,
                )
                for h in range(f * heads_out, (f + 1) * heads_out)
            ],
            axis=1,
        )
    mine = lax.axis_index("ffn")
    for f in range(peers):
        outs[f][...] = shares[mine ^ f].astype(BF16)
    for load in loads[2 * slots :]:
        load.wait()


def stack(count, *refs):
    out = refs[-1]
    for i, ref in enumerate(refs[:count]):
        out[i] = ref[...]


def add(count, *refs):
    total = refs[0][...].astype(F32)
    for ref in refs[1:count]:
        total += ref[...].astype(F32)
    refs[-1][...] = total.astype(BF16)


def project(slots, peers, slot_of, weight, *refs):
    refs, outs, table_out = refs[:-peers], refs[-peers:-1], refs[-1]
    requests = slot_of.shape[1]
    _, rows, width = refs[0].shape
    kv_here = weight.shape[0]
    table = [ref[...].astype(F32).reshape(ref.shape[0] * rows, width) for ref in refs]
    table = jnp.concatenate(table, axis=0).astype(BF16)
    slot = slot_of[...]
    mine = lax.axis_index(("tok", "ffn"))
    where_from = ((slot // slots) ^ mine) * rows + lax.rem(slot, slots)
    row = lax.broadcasted_iota(jnp.int32, (table.shape[0], requests), 0)
    for g in range(kv_here):
        pick = (row == where_from + g * slots).astype(F32).astype(BF16)
        table_out[g] = lax.dot_general(
            pick, table, (((0,), (0,)), ((), ())), preferred_element_type=F32
        ).astype(BF16)
    for p, out in enumerate(outs):
        project_part(p + 1, table_out, weight, out)


def project_part(peer, ordered, weight, out):
    width = out.shape[1]
    step = column_step(width)
    first = (lax.axis_index("rep") ^ peer) * width
    for c in range(0, width, step):
        at = pl.ds(pl.multiple_of(first + c, 128), step)
        total = jnp.zeros((out.shape[0], step), F32)
        for g in range(weight.shape[0]):
            total += jnp.dot(ordered[g], weight[g, :, at], preferred_element_type=F32)
        out[:, c : c + step] = total.astype(BF16)


def by_owner(value, ordered):
    blocks, rows, _ = ordered.shape
    mine = lax.axis_index("tok")
    for k in range(blocks):
        ordered[k] = value[k * rows : (k + 1) * rows]
    return jnp.concatenate([ordered[mine ^ k] for k in range(blocks)], axis=0)


def part_rows(peer, height):
    return pl.ds(pl.multiple_of((lax.axis_index("rep") ^ peer) * height, height), height)


def own_part(core, mid, gain, weight, left, sums, ordered):
    @pl.when(lax.axis_index("rep") == core)
    def _():
        scaled = mid[...].astype(F32) * gain[core]
        rhs = by_owner(scaled, ordered).astype(BF16)
        left[...] = rhs
        height = mid.shape[1]
        step = column_step(weight.shape[1])
        for c in range(0, weight.shape[1], step):
            sums[:, c : c + step] = jnp.dot(
                rhs,
                weight[core * height : (core + 1) * height, c : c + step],
                preferred_element_type=F32,
            )


def gate_first(core, residual, gain, weight, later, *refs):
    mid, left, sums, ordered = refs[-4:]
    total = residual[lax.axis_index("rep")].astype(F32)
    for ref in refs[:-4]:
        total += ref[...].astype(F32)
    mid[...] = total.astype(BF16)
    own_part(core, mid, gain, weight, left, sums, ordered)


def gate_next(core, mid, gain, weight, left_in, sums_in, left, sums, ordered):
    own_part(core, mid, gain, weight, left, sums, ordered)


def up_own(left, weight, sums):
    rhs = left[...]
    at = part_rows(0, left.shape[1])
    step = column_step(weight.shape[1])
    for c in range(0, weight.shape[1], step):
        sums[:, c : c + step] = jnp.dot(
            rhs, weight[at, c : c + step], preferred_element_type=F32
        )


def gate_rest(peers, *refs):
    mids = refs[:peers]
    gain, weight, sums, mid_out, left, stat_out, out, ordered, squares = refs[peers:]
    blocks, rows, height = ordered.shape
    core = lax.axis_index("rep")
    share = mid_out.shape[2]
    square = jnp.zeros((blocks * rows, 1), F32)
    lefts = []
    for p in range(peers):
        mid = mids[p][...].astype(F32)
        for j in range(mid_out.shape[1]):
            mid_out[core ^ p, j] = mid[j * share : (j + 1) * share].astype(BF16)
        square += jnp.sum(mid * mid, axis=1, keepdims=True)
        if p > 0:
            scaled = by_owner(mid * gain[core ^ p], ordered).astype(BF16)
            left[p - 1] = scaled
            lefts.append(scaled)
    square = by_owner(jnp.broadcast_to(square, (blocks * rows, 128)), squares)
    high = square.astype(BF16).astype(F32)
    medium = (square - high).astype(BF16).astype(F32)
    low = square - high - medium
    lane = lax.broadcasted_iota(jnp.int32, square.shape, 1)
    stat = jnp.where(lane == 0, high, jnp.where(lane == 1, medium, low))
    stat = jnp.where(lane < 3, stat, 0.0).astype(BF16)
    for k in range(blocks):
        stat_out[k] = stat[k * rows : (k + 1) * rows]
    width = weight.shape[1]
    step = column_step(width)
    for c in range(0, width, step):
        total = sums[:, c : c + step]
        for p in range(1, peers):
            total += jnp.dot(
                lefts[p - 1],
                weight[part_rows(p, height), c : c + step],
                preferred_element_type=F32,
            )
        for k in range(blocks):
            out[k, :, c : c + step] = total[k * rows : (k + 1) * rows].astype(BF16)


def up_rest(sums, rest, stat, gates, weight, *parts):
    rows = parts[0].shape[0]
    height, width = rest.shape[2], weight.shape[1]
    for k, part in enumerate(parts):
        part[:, :width] = gates[k]
        part[:, 2 * width :] = stat[k]
    lefts = [rest[p] for p in range(rest.shape[0])]
    step = column_step(width)
    for c in range(0, width, step):
        total = sums[:, c : c + step]
        for p, left in enumerate(lefts):
            total += jnp.dot(
                left, weight[part_rows(p + 1, height), c : c + step], preferred_element_type=F32
            )
        for k, part in enumerate(parts):
            part[:, width + c : width + c + step] = total[k * rows : (k + 1) * rows].astype(BF16)


def activate(features, *refs):
    out = refs[-1]
    width = out.shape[1]
    total = refs[0][...].astype(F32)
    for part in refs[1:-1]:
        total += part[...].astype(F32)
    square = jnp.sum(total[:, 2 * width :], axis=1, keepdims=True)
    inv_rms = lax.rsqrt(square / features + 1e-05)
    gate = total[:, :width] * inv_rms
    up = total[:, width : 2 * width] * inv_rms
    out[...] = (gate / (1.0 + jnp.exp(-gate)) * up).astype(BF16)


def down(blocks, pieces, *refs):
    parts = refs[:blocks]
    weights = refs[blocks : blocks + pieces]
    outs = refs[blocks + pieces : -1]
    ordered = refs[-1]
    mine, group = lax.axis_index("tok"), lax.axis_index(("ffn", "rep"))
    rows = parts[0].shape[0]
    share = outs[0].shape[0]
    for k in range(blocks):
        at = pl.multiple_of((mine ^ k) * rows, 8)
        ordered[pl.ds(at, rows)] = parts[k][...].astype(F32)
    left = jnp.concatenate(
        [
            ordered[pl.ds(pl.multiple_of((group ^ j) * share, 8), share)]
            for j in range(len(outs))
        ],
        axis=0,
    ).astype(BF16)
    base = 0
    for weight in weights:
        width = weight.shape[1]
        step = column_step(width)
        for c in range(0, width, step):
            total = jnp.dot(left, weight[:, c : c + step], preferred_element_type=F32)
            for j, out in enumerate(outs):
                at = base + c
                out[:, at : at + step] = total[j * share : (j + 1) * share].astype(BF16)
        base += width


def finish(mid, *refs):
    mine = lax.axis_index(("ffn", "rep"))
    out = refs[-1]
    total = jnp.concatenate([mid[p, mine] for p in range(mid.shape[0])], axis=1).astype(F32)
    for part in refs[:-1]:
        total += part[...].astype(F32)
    out[...] = total.astype(BF16)


def like(*shape):
    return jax.ShapeDtypeStruct(shape, BF16)


def limit(mib):
    return pltpu.CompilerParams(vmem_limit_bytes=mib * MIB)


def shards(
    queries,
    new_key,
    new_value,
    key_cache,
    value_cache,
    lengths,
    slot_of,
    residual_in,
    out_weight,
    norm_gain,
    gate_weight,
    up_weight,
    down_weight,
):
    tok, ffn, rep = (lax.axis_size(a) for a in ("tok", "ffn", "rep"))
    sums = ffn * rep
    slots, span, kv_width = key_cache.shape
    kv_here = kv_width // HEAD_DIM
    requests, features = residual_in.shape
    hidden_here = gate_weight.shape[1]
    feat_width = out_weight.shape[1]
    in_hbm = functools.partial(pltpu.with_memory_space_constraint, memory_space=pltpu.HBM)

    height = features // rep
    slot_of = slot_of.reshape(1, requests)
    carried = [
        slot_of,
        residual_in,
        norm_gain.reshape(1, features),
    ]
    table_rows = slots * kv_here
    *attended, slot_of, residual_in, norm_gain = pl.pallas_call(
        functools.partial(attend, ffn),
        out_shape=[like(table_rows, feat_width)] * ffn
        + [
            pltpu.VMEM(slot_of.shape, slot_of.dtype),
            pltpu.VMEM((rep, requests, height), BF16),
            pltpu.VMEM((rep, 1, height), F32),
        ],
        in_specs=[HBM] * (6 + len(carried)),
        out_specs=[VMEM] * (ffn + len(carried)),
        scratch_shapes=[
            pltpu.SMEM(lengths.shape, jnp.int32),
            pltpu.VMEM(queries.shape, BF16),
            pltpu.VMEM(new_key.shape, BF16),
            pltpu.VMEM(new_value.shape, BF16),
            pltpu.VMEM(key_cache.shape, BF16),
            pltpu.VMEM(value_cache.shape, BF16),
            pltpu.VMEM((ffn, table_rows, feat_width), F32),
            pltpu.SemaphoreType.DMA((5 + 2 * slots + 2 * rep,)),
        ],
        compiler_params=limit(3),
        cost_estimate=pl.CostEstimate(flops=20000000000, transcendentals=0, bytes_accessed=0),
        name="attend",
    )(
        *(
            in_hbm(a)
            for a in [lengths, queries, new_key, new_value, key_cache, value_cache] + carried
        )
    )
    owners = tok * ffn
    near = min(2, tok)
    out_weight = pltpu.with_memory_space_constraint(out_weight, pltpu.VMEM)
    in_vmem = functools.partial(pltpu.with_memory_space_constraint, memory_space=pltpu.VMEM)
    close = [None] * (near * ffn)
    for k in reversed(range(near * ffn)):
        close[k] = lax.ppermute(
            attended[k % ffn], ("tok", "ffn", "rep"), swap(owners * rep, k * rep + rep - 1)
        )
    gate_weight = in_vmem(gate_weight)
    close = pl.pallas_call(
        functools.partial(stack, near * ffn),
        out_shape=like(near * ffn, table_rows, feat_width),
        in_specs=[VMEM] * (near * ffn + 1),
        out_specs=VMEM,
        compiler_params=limit(3),
        name="stack",
    )(*close, gate_weight)
    gathered = [
        lax.ppermute(close, ("tok", "rep"), swap(tok * rep, k * rep + rep - 1))
        for k in range(0, tok, near)
    ]

    *given, ordered = pl.pallas_call(
        functools.partial(project, slots, rep),
        out_shape=[like(requests, height)] * (rep - 1) + [like(kv_here, requests, feat_width)],
        in_specs=[VMEM] * (2 + len(gathered)),
        out_specs=[VMEM] * rep,
        compiler_params=limit(3),
        cost_estimate=pl.CostEstimate(flops=10000000000, transcendentals=0, bytes_accessed=0),
        name="project",
    )(slot_of, out_weight, *gathered)
    summed = [lax.ppermute(part, "rep", swap(rep, k + 1)) for k, part in enumerate(given)]
    kept = pl.pallas_call(
        functools.partial(project_part, 0),
        out_shape=like(requests, height),
        in_specs=[VMEM] * 2,
        out_specs=VMEM,
        compiler_params=limit(3),
        name="project_own",
    )(ordered, out_weight)
    summed = [kept] + summed
    here = pl.pallas_call(
        functools.partial(add, len(summed)),
        out_shape=like(requests, height),
        in_specs=[VMEM] * len(summed),
        out_specs=VMEM,
        compiler_params=limit(3),
        name="add",
    )(*summed)
    arrived = [lax.ppermute(here, "ffn", swap(ffn, k)) for k in range(1, ffn)]
    rows = requests // tok
    share = requests // sums
    up_weight = in_vmem(up_weight)
    own_shapes = [like(requests, height), jax.ShapeDtypeStruct((requests, hidden_here), F32)]
    mid_own, own, own_sums = pl.pallas_call(
        functools.partial(gate_first, rep - 1),
        out_shape=[like(requests, height)] + own_shapes,
        in_specs=[VMEM] * (4 + ffn),
        out_specs=[VMEM] * 3,
        scratch_shapes=[pltpu.VMEM((tok, rows, height), F32)],
        compiler_params=limit(3),
        name="gate_first",
    )(residual_in, norm_gain, gate_weight, up_weight, here, *arrived)
    mids = [mid_own] + [lax.ppermute(mid_own, "rep", swap(rep, k)) for k in range(1, rep)]
    for core in reversed(range(rep - 1)):
        own, own_sums = pl.pallas_call(
            functools.partial(gate_next, core),
            out_shape=own_shapes,
            in_specs=[VMEM] * 5,
            out_specs=[VMEM] * 2,
            input_output_aliases={3: 0, 4: 1},
            scratch_shapes=[pltpu.VMEM((tok, rows, height), F32)],
            compiler_params=limit(3),
            name="gate_next",
        )(mid_own, norm_gain, gate_weight, own, own_sums)
    up_sums = pl.pallas_call(
        up_own,
        out_shape=own_shapes[1],
        in_specs=[VMEM] * 2,
        out_specs=VMEM,
        compiler_params=limit(3),
        name="up_own",
    )(own, up_weight)
    mid, rest, stat, gates = pl.pallas_call(
        functools.partial(gate_rest, rep),
        out_shape=[
            like(rep, sums, share, height),
            like(rep - 1, requests, height),
            like(tok, rows, 128),
            like(tok, rows, hidden_here),
        ],
        in_specs=[VMEM] * (3 + rep),
        out_specs=[VMEM] * 4,
        scratch_shapes=[
            pltpu.VMEM((tok, rows, height), F32),
            pltpu.VMEM((tok, rows, 128), F32),
        ],
        compiler_params=limit(3),
        name="gate_rest",
    )(*mids, norm_gain, gate_weight, own_sums)
    parts = pl.pallas_call(
        up_rest,
        out_shape=[like(rows, 2 * hidden_here + 128)] * tok,
        in_specs=[VMEM] * 5,
        out_specs=[VMEM] * tok,
        compiler_params=limit(3),
        name="up_rest",
    )(up_sums, rest, stat, gates, up_weight)
    order = sorted(range(1, tok), reverse=True)
    got = [parts[0]] + [lax.ppermute(parts[k], "tok", swap(tok, k)) for k in order]

    hidden = pl.pallas_call(
        functools.partial(activate, features * tok),
        out_shape=like(rows, hidden_here),
        in_specs=[VMEM] * tok,
        out_specs=VMEM,
        compiler_params=limit(3),
        name="activate",
    )(*got)
    pieces = {k: lax.ppermute(hidden, "tok", swap(tok, k)) for k in sorted(range(1, tok), reverse=True)}

    downs = pl.pallas_call(
        functools.partial(down, tok, 1),
        out_shape=[like(share, features)] * sums,
        in_specs=[VMEM] * (1 + tok),
        out_specs=[VMEM] * sums,
        scratch_shapes=[pltpu.VMEM((requests, hidden_here), F32)],
        compiler_params=limit(3),
        name="down",
    )(hidden, *[pieces[k] for k in range(1, tok)], in_vmem(down_weight))
    order = sorted(range(1, sums), reverse=True)
    got = [downs[0]] + [lax.ppermute(downs[j], ("ffn", "rep"), swap(sums, j)) for j in order]

    return pl.pallas_call(
        finish,
        out_shape=like(share, features),
        in_specs=[VMEM] * (1 + sums),
        out_specs=VMEM,
        compiler_params=limit(3),
        name="finish",
    )(mid, *got)


def solution(mesh):
    placed = (
        P(("groups", "tok", "ffn"), "rep"),
        P(("groups", "tok", "ffn"), "rep"),
        P(("groups", "tok", "ffn"), "rep"),
        P(("groups", "tok", "ffn"), None, "rep"),
        P(("groups", "tok", "ffn"), None, "rep"),
        P(("groups", "tok", "ffn")),
        P("groups"),
        P("groups", "tok"),
        P("rep", "ffn", "tok"),
        P("tok"),
        P("tok", ("ffn", "rep")),
        P("tok", ("ffn", "rep")),
        P(("ffn", "rep"), "tok"),
    )
    return jax.shard_map(
        shards,
        mesh=mesh,
        in_specs=placed,
        out_specs=P(("groups", "ffn", "rep"), "tok"),
        check_vma=False,
    )
```
